256 devices in a mesh: region: 32 (over y, z_lo, core), factor: 8 (over x, z_hi).
Axes of the slice: x: 4, y: 4, z: 8 (z_hi: 2, z_lo: 4; z = z_hi * 4 + z_lo), core: 2. Of those that a mesh axis runs over, the one named last changes fastest.
Arguments:
- response: bfloat16 [2000, 262144], P('factor', 'region'), may hold values from -6 to 6
- loadings: float32 [2000, 8], replicated, may hold values from -6 to 6
- obs_count: int32 [2000], replicated, may hold values from 1 to 16
- couplings: float32 [8, 2048, 2], P('factor', 'region'), may hold values from 0.3 to 0.9
- block_cov: float32 [8, 2048, 128, 128], P('factor', 'region'), may hold values from -0.07 to 0.5
- noise_factor: float32 [8, 2048, 128, 128], P('factor', 'region'), may hold values from -0.09 to 0.65
- noise: float32 [8, 262144], P('factor', 'region'), may hold values from -6 to 6
- latents: float32 [8, 262144], P('factor', 'region'), may hold values from -6 to 6
- colours: int32 [64], P('region'), may hold values from 0 to 3
- partners: int32 [64, 2], P('region'), may hold values from 0 to 63, as said below
Outputs:
- new_latents: float32 [8, 262144], P('factor', 'region')
The draws below stay inside these ranges and needn't reach their ends.
Inputs may be any that keep to these rules, and one draw needn't show every extreme that they name: Column 1 of partners is a permutation of the regions, and partners[partners[g, 1], 0] = g for every region g.
All inputs are finite; a program needn't handle non-finite values.
Results may differ from the reference program's by a relative error of at most 0.00088.
Values sent between devices are 32-bit elements; how exact they have to be, the bound alone decides.
A program may use at most 64 MiB of HBM per device.

```python
import math
import jax
import jax.numpy as jnp
from jax import lax

FACTORS = 8
SPECIES = 2000
RSITES = 4096
BLK = 128
COLOURS = 4
NREG = 64
BPR = 32
NBLOCKS = 2048
SITES = 262144


def combine_blocks(diagonal, spread_part):
    eye_mask = jnp.eye(BLK, dtype=jnp.float32)
    return spread_part * (1.0 - eye_mask) + diagonal[..., None] * eye_mask


def draw_block_cov(key, part):
    key = jax.random.fold_in(key, 11)
    diagonal_key, spread_key = jax.random.split(key)
    full_shape = (FACTORS, NBLOCKS, BLK, BLK)
    spread = 0.15 / BLK ** 0.5
    diagonal = jax.random.uniform(diagonal_key, (FACTORS, NBLOCKS, BLK), jnp.float32, 0.15, 0.45)
    spread_part = jax.random.uniform(spread_key, full_shape, jnp.float32, -1.7, 1.7) * spread
    return combine_blocks(diagonal, spread_part).astype(jnp.float32)


def draw_noise_factor(key, part):
    key = jax.random.fold_in(key, 23)
    diagonal_key, spread_key = jax.random.split(key)
    full_shape = (FACTORS, NBLOCKS, BLK, BLK)
    spread = 0.2 / BLK ** 0.5
    diagonal = jax.random.uniform(diagonal_key, (FACTORS, NBLOCKS, BLK), jnp.float32, 0.3, 0.6)
    spread_part = jax.random.uniform(spread_key, full_shape, jnp.float32, -1.7, 1.7) * spread
    return combine_blocks(diagonal, spread_part).astype(jnp.float32)


def draw_partners(key, part):
    key = jax.random.fold_in(key, 37)
    forward = jax.random.permutation(key, NREG).astype(jnp.int32)
    inverse = jnp.argsort(forward, stable=True).astype(jnp.int32)
    return jnp.stack([inverse, forward], axis=1)


def plant(entries, stream_key, least, top_value):
    shape = entries.shape
    index_at = [jax.random.randint(jax.random.fold_in(stream_key, axis), (), 0, shape[axis]) for axis in range(len(shape))]
    entries = entries.at[tuple(index_at)].set(least)
    longest = shape.index(max(shape))
    index_at[longest] = (index_at[longest] + 1) % shape[longest]
    return entries.at[tuple(index_at)].set(top_value)


def block_levels(rng, shape, cuts, least, largest):
    gain, own = 1.0, jax.random.fold_in(rng, 6)
    for position, shards_of in cuts:
        steps = jnp.exp(jax.random.uniform(jax.random.fold_in(own, position), (shards_of,), jnp.float32, least / len(cuts), largest / len(cuts)))
        gain = gain * jnp.repeat(steps, shape[position] // shards_of).reshape([-1 if axis == position else 1 for axis in range(len(shape))])
    return gain


def bell_draw(stream_key, dims, scale, bound, cuts=(), kind=jnp.bfloat16):
    gain = block_levels(stream_key, dims, cuts, -0.22, 0.18) if cuts else 1.0
    values = jax.random.normal(stream_key, dims, jnp.float32) * scale * gain
    return jnp.minimum(jnp.maximum(values, -bound), bound).astype(kind)


def setup_inputs(seed: int = 0) -> dict:
    key_of = jax.random.split(jax.random.key(seed), 11)
    response = bell_draw(key_of[0], (SPECIES, SITES), 1.0, 6.0, ((0, 8), (1, 32)))
    loadings = bell_draw(key_of[1], (SPECIES, FACTORS), 1.0, 6.0, (), jnp.float32)
    obs_count = plant(jax.random.randint(key_of[2], (SPECIES,), 1, 17), jax.random.fold_in(key_of[2], 1), 1, 16).astype(jnp.int32)
    couplings = jnp.clip(0.3 + 0.59999996 * jax.random.uniform(key_of[3], (FACTORS, NBLOCKS, 2), jnp.float32) ** block_levels(key_of[3], (FACTORS, NBLOCKS, 2), ((0, 8), (1, 32)), -0.2, 0.2), 0.3, 0.9)
    block_cov = draw_block_cov(jax.random.fold_in(key_of[10], 71), 0)
    noise_factor = draw_noise_factor(jax.random.fold_in(key_of[10], 71), 0)
    noise = bell_draw(key_of[6], (FACTORS, SITES), 1.0, 6.0, ((0, 8), (1, 32)), jnp.float32)
    latents = bell_draw(key_of[7], (FACTORS, SITES), 1.0, 6.0, ((0, 8), (1, 32)), jnp.float32)
    colours = plant(jax.random.randint(key_of[8], (NREG,), 0, COLOURS), jax.random.fold_in(key_of[8], 1), 0, COLOURS - 1).astype(jnp.int32)
    partners = draw_partners(jax.random.fold_in(key_of[10], 71), 0)
    return dict(response=response, loadings=loadings, obs_count=obs_count, couplings=couplings, block_cov=block_cov, noise_factor=noise_factor, noise=noise, latents=latents, colours=colours, partners=partners)


def apply_blocks(matrices, vectors):
    return jnp.einsum('...ij,...j->...i', matrices, vectors, precision=lax.Precision.HIGHEST)

def reference(response, loadings, obs_count, couplings, block_cov, noise_factor, noise, latents, colours, partners):
    weights = obs_count.astype(jnp.float32) * (0.25 / math.sqrt(SPECIES))
    weighted = loadings * weights[:, None]
    gram_matrix = jnp.dot(weighted.T, loadings, precision=lax.Precision.HIGHEST)
    offdiag = gram_matrix * (1.0 - jnp.eye(FACTORS, dtype=jnp.float32))
    data_term = jnp.dot(weighted.astype(jnp.bfloat16).T, response, preferred_element_type=jnp.float32)
    coupled = couplings.reshape(FACTORS, NREG, BPR, 2)
    noise_draw = apply_blocks(noise_factor, noise.reshape(FACTORS, NBLOCKS, BLK))
    site_colour = jnp.repeat(colours, RSITES)
    current = latents
    for phase_index in range(COLOURS):
        cross = jnp.dot(offdiag, current, precision=lax.Precision.HIGHEST)
        blocks = current.reshape(FACTORS, NREG, BPR, BLK)
        left_edge = blocks[:, partners[:, 0], BPR - 1]
        right_edge = blocks[:, partners[:, 1], 0]
        left_block = jnp.concatenate([left_edge[:, :, None], blocks[:, :, :-1]], axis=2)
        right_block = jnp.concatenate([blocks[:, :, 1:], right_edge[:, :, None]], axis=2)
        field_term = (data_term - cross).reshape(FACTORS, NREG, BPR, BLK)
        field_term = field_term + coupled[..., 0:1] * left_block + coupled[..., 1:2] * right_block
        sample = apply_blocks(block_cov, field_term.reshape(FACTORS, NBLOCKS, BLK)) + noise_draw
        current = jnp.where(site_colour[None, :] == phase_index, sample.reshape(FACTORS, SITES), current)
    return current
```

```python
import functools
import math

import jax
import jax.numpy as jnp
from jax import lax
from jax.experimental import pallas as pl
from jax.experimental.pallas import tpu as pltpu
from jax.sharding import PartitionSpec as P

MESH = pl.DeviceIdType.MESH
LANES = 128
CHUNKS = (
    ((0, 4), (28, 8), (60, 4)),
    ((4, 16),),
    ((20, 8), (36, 8)),
    ((44, 16),),
)
PER_CHUNK = 16
ENDS = (0, 7, 8, 15)


def kernel(
    species_total,
    resp_hbm,
    load_hbm,
    obs_hbm,
    coup_hbm,
    cov_hbm,
    nf_hbm,
    noise_hbm,
    lat_hbm,
    col_hbm,
    par_hbm,
    out_ref,
    resp_v,
    load_v,
    obs_v,
    coup_v,
    cov_v,
    nf_v,
    noise_v,
    lat_v,
    col_s,
    par_s,
    draw_v,
    local_v,
    field_v,
    c0_v,
    c1_v,
    part_v,
    x_recv,
    z_send,
    z_recv,
    keep_v,
    old_v,
    new_v,
    small_sem,
    resp_sem,
    nf_sem,
    cov_sem,
    x_ssem,
    x_rsem,
    z_ssem,
    z_rsem,
    old_ssem,
    old_rsem,
    new_ssem,
    new_rsem,
):
    n_chunks = len(CHUNKS)
    factors = load_v.shape[0]
    species_local = resp_v.shape[1]
    region_n = lax.axis_size("region")
    ri = lax.axis_index("region")
    fi = lax.axis_index("factor")
    xi = fi // 2
    zi = fi % 2

    small = [
        pltpu.make_async_copy(src, dst, small_sem.at[i])
        for i, (src, dst) in enumerate(
            (
                (load_hbm, load_v),
                (obs_hbm, obs_v),
                (lat_hbm, lat_v),
                (coup_hbm, coup_v),
                (noise_hbm, noise_v),
                (col_hbm, col_s),
                (par_hbm, par_s),
            )
        )
    ]
    for copy in small:
        copy.start()
    resp_in, nf_in, cov_in = [], [], []
    for c, runs in enumerate(CHUNKS):
        at, rows = 0, []
        for i, (first, count) in enumerate(runs):
            rows.append(
                pltpu.make_async_copy(
                    resp_hbm.at[:, pl.ds(first * LANES, count * LANES)],
                    resp_v.at[c, :, pl.ds(at * LANES, count * LANES)],
                    resp_sem.at[c, i],
                )
            )
            at += count
        resp_in.append(rows)
    for hbm, ref, sem, out in ((nf_hbm, nf_v, nf_sem, nf_in), (cov_hbm, cov_v, cov_sem, cov_in)):
        for c, runs in enumerate(CHUNKS):
            at, rows = c * PER_CHUNK, []
            for i, (first, count) in enumerate(runs):
                rows.append(
                    pltpu.make_async_copy(
                        hbm.at[pl.ds(first, count)], ref.at[pl.ds(at, count)], sem.at[c, i]
                    )
                )
                at += count
            out.append(rows)
    for group in (resp_in, nf_in, cov_in):
        for rows in group:
            for copy in rows:
                copy.start()

    x_peers = [lax.rem(xi + d, 4) * 2 + zi for d in (1, 2, 3)]
    z_peer = xi * 2 + (1 - zi)
    barrier = pltpu.get_barrier_semaphore()
    for peer in x_peers + [z_peer]:
        pl.semaphore_signal(barrier, inc=1, device_id={"factor": peer}, device_id_type=MESH)

    @pl.loop(1, region_n)
    def _(d):
        pl.semaphore_signal(
            barrier, inc=1, device_id={"region": lax.rem(ri + d, region_n)}, device_id_type=MESH
        )

    small[0].wait()
    small[1].wait()
    tau = obs_v[...].astype(jnp.float32) * (0.25 / math.sqrt(species_total))
    weighted = load_v[...] * tau
    own_load = load_v[pl.ds(fi, 1), :]
    gram = jnp.sum(weighted * own_load, axis=1, keepdims=True)
    gram = jnp.where(lax.broadcasted_iota(jnp.int32, gram.shape, 0) == fi, 0.0, gram)
    mine = weighted[:, :species_local]
    for k in range(1, factors):
        mine = jnp.where(fi == k, weighted[:, k * species_local : (k + 1) * species_local], mine)
    mine = mine.astype(jnp.bfloat16)
    gram = jnp.broadcast_to(gram, (factors, LANES))

    small[2].wait()
    small[5].wait()
    nb = lat_v.shape[0]
    half = nb // 2
    old_v[ri, pl.ds(0, 1), :] = lat_v[0:1, :]
    old_v[ri, pl.ds(1, 1), :] = lat_v[half - 1 : half, :]
    old_v[ri, pl.ds(2, 1), :] = lat_v[half : half + 1, :]
    old_v[ri, pl.ds(3, 1), :] = lat_v[nb - 1 : nb, :]
    for q in range(2):
        old_v[ri, pl.ds(4 + q, 1), :] = jnp.full((1, LANES), col_s[q].astype(jnp.float32))

    def partial_term(c):
        for copy in resp_in[c]:
            copy.wait()
        term = jnp.dot(mine, resp_v[c], preferred_element_type=jnp.float32)
        at = 0
        for first, count in CHUNKS[c]:
            for k in range(count):
                row = lat_v[first + k : first + k + 1, :]
                value = term[:, at * LANES : (at + 1) * LANES] - gram * row
                part_v[c, pl.ds(at, factors, stride=PER_CHUNK), :] = value
                at += 1

    def x_copies(c):
        copies = []
        for d in range(3):
            start = pl.multiple_of((x_peers[d] - zi) * PER_CHUNK, 2 * PER_CHUNK)
            copies.append(
                pltpu.make_async_remote_copy(
                    src_ref=part_v.at[c, pl.ds(start, 2 * PER_CHUNK)],
                    dst_ref=x_recv.at[c, d],
                    send_sem=x_ssem.at[c, d],
                    recv_sem=x_rsem.at[c, d],
                    device_id={"factor": x_peers[d]},
                    device_id_type=MESH,
                )
            )
        return copies

    def z_copy(c):
        return pltpu.make_async_remote_copy(
            src_ref=z_send.at[c],
            dst_ref=z_recv.at[c],
            send_sem=z_ssem.at[c],
            recv_sem=z_rsem.at[c],
            device_id={"factor": z_peer},
            device_id_type=MESH,
        )

    def send_all(buf, ssem, rsem):
        @pl.loop(1, region_n)
        def _(d):
            pltpu.make_async_remote_copy(
                src_ref=buf.at[ri],
                dst_ref=buf.at[ri],
                send_sem=ssem,
                recv_sem=rsem,
                device_id={"region": lax.rem(ri + d, region_n)},
                device_id_type=MESH,
            ).start()

    def wait_all(buf, sem):
        others = buf.at[pl.ds(0, region_n - 1)]
        pltpu.make_async_copy(others, others, sem).wait()

    partial_term(0)
    pl.semaphore_wait(barrier, 4 + region_n - 1)
    xs = [x_copies(c) for c in range(n_chunks)]
    zs = [z_copy(c) for c in range(n_chunks)]
    for copy in xs[0]:
        copy.start()
    send_all(old_v, old_ssem, old_rsem)
    for c in range(1, n_chunks):
        partial_term(c)
        for copy in xs[c]:
            copy.start()

    diagonal = lax.broadcasted_iota(jnp.int32, (LANES, LANES), 0) == lax.broadcasted_iota(
        jnp.int32, (LANES, LANES), 1
    )

    def times(matrix, row):
        sums = jnp.sum(matrix * row, axis=1, keepdims=True)
        return jnp.sum(jnp.where(diagonal, sums, 0.0), axis=0, keepdims=True)

    small[3].wait()
    pick = lax.broadcasted_iota(jnp.int32, (nb, nb), 0) == lax.broadcasted_iota(
        jnp.int32, (nb, nb), 1
    )
    for i, ref in ((0, c0_v), (1, c1_v)):
        column = jnp.sum(jnp.where(pick, coup_v[i : i + 1, :], 0.0), axis=1, keepdims=True)
        ref[...] = jnp.broadcast_to(column, (nb, LANES))
    rows_at = lax.broadcasted_iota(jnp.int32, (nb, LANES), 0)
    left = pltpu.roll(lat_v[...], 1, 0)
    left = jnp.where((rows_at == 0) | (rows_at == half), 0.0, left)
    right = pltpu.roll(lat_v[...], nb - 1, 0)
    right = jnp.where((rows_at == half - 1) | (rows_at == nb - 1), 0.0, right)
    local_v[...] = c0_v[...] * left + c1_v[...] * right
    small[4].wait()

    def draw(c):
        for copy in nf_in[c]:
            copy.wait()
        at = c * PER_CHUNK
        for first, count in CHUNKS[c]:

            @pl.loop(0, count // 4)
            def _(g, at=at, first=first):
                for k in range(4):
                    row = noise_v[pl.ds(first + 4 * g + k, 1), :]
                    draw_v[pl.ds(first + 4 * g + k, 1), :] = times(nf_v[at + 4 * g + k], row)

            at += count

    def x_sum(c):
        for copy in xs[c]:
            copy.wait_recv()
        at = pl.multiple_of(fi * PER_CHUNK, PER_CHUNK)
        to = pl.multiple_of(z_peer * PER_CHUNK, PER_CHUNK)
        mine_at = pl.multiple_of(zi * PER_CHUNK, PER_CHUNK)
        other_at = pl.multiple_of((1 - zi) * PER_CHUNK, PER_CHUNK)
        out = part_v[c, pl.ds(to, PER_CHUNK), :]
        for d in range(3):
            out = out + x_recv[c, d, pl.ds(other_at, PER_CHUNK), :]
        z_send[c] = out
        zs[c].start()
        own = part_v[c, pl.ds(at, PER_CHUNK), :]
        for d in range(3):
            own = own + x_recv[c, d, pl.ds(mine_at, PER_CHUNK), :]
        keep_v[c] = own

    def z_sum(c):
        zs[c].wait_recv()
        total = keep_v[c] + z_recv[c]
        at = 0
        for first, count in CHUNKS[c]:
            field_v[first : first + count, :] = (
                total[at : at + count, :] + local_v[first : first + count, :]
            )
            at += count

    def blocks(c):
        for copy in cov_in[c]:
            copy.wait()
        at = c * PER_CHUNK
        for first, count in CHUNKS[c]:

            @pl.loop(0, count // 4)
            def _(g, at=at, first=first):
                for k in range(4):
                    b = first + 4 * g + k
                    row = field_v[pl.ds(b, 1), :]
                    out_ref[pl.ds(b, 1), :] = (
                        times(cov_v[at + 4 * g + k], row) + draw_v[pl.ds(b, 1), :]
                    )

            at += count

    def partner_edge(ref, q, side):
        g = par_s[q, side]
        return ref[g // 2, pl.ds(2 * (g % 2) + (1 - side), 1), :]

    def partner_colour(q, side):
        g = par_s[q, side]
        return old_v[g // 2, pl.ds(4 + g % 2, 1), :]

    ends = [
        (q, side, (q * half, q * half + half - 1)[side], ENDS[2 * q + side])
        for q in range(2)
        for side in range(2)
    ]

    draw(0)
    x_sum(0)
    draw(1)
    x_sum(1)
    draw(2)
    z_sum(0)
    small[6].wait()
    for copy in cov_in[0]:
        copy.wait()
    wait_all(old_v, old_rsem)
    for q, side, b, at in ends:
        weight = (c0_v, c1_v)[side][b : b + 1, :]
        row = field_v[b : b + 1, :] + weight * partner_edge(old_v, q, side)
        new_v[ri, pl.ds(2 * q + side, 1), :] = times(cov_v[at], row) + draw_v[b : b + 1, :]
    send_all(new_v, new_ssem, new_rsem)
    x_sum(2)
    draw(3)
    x_sum(3)
    cov_in[0] = []
    for c in range(n_chunks):
        if c:
            z_sum(c)
        blocks(c)
    wait_all(new_v, new_rsem)
    for q, side, b, at in ends:
        weight = (c0_v, c1_v)[side][b : b + 1, :]
        own = jnp.full((1, LANES), col_s[q].astype(jnp.float32))
        edge = jnp.where(
            partner_colour(q, side) < own,
            partner_edge(new_v, q, side),
            partner_edge(old_v, q, side),
        )
        row = field_v[b : b + 1, :] + weight * edge
        out_ref[b : b + 1, :] = times(cov_v[at], row) + draw_v[b : b + 1, :]

    for c in range(n_chunks):
        for copy in xs[c]:
            copy.wait_send()
        zs[c].wait_send()
    wait_all(old_v, old_ssem)
    wait_all(new_v, new_ssem)


def on_device(
    response,
    loadings,
    obs_count,
    couplings,
    block_cov,
    noise_factor,
    noise,
    latents,
    colours,
    partners,
):
    f32 = jnp.float32
    factors = loadings.shape[1]
    species = loadings.shape[0]
    nb = block_cov.shape[1]
    region_n = lax.axis_size("region")
    n_chunks = len(CHUNKS)
    runs = max(len(c) for c in CHUNKS)
    any_spec = pl.BlockSpec(memory_space=pl.ANY)
    dma = pltpu.SemaphoreType.DMA
    out = pl.pallas_call(
        functools.partial(kernel, species),
        out_shape=jax.ShapeDtypeStruct((nb, LANES), f32),
        in_specs=[any_spec] * 10,
        out_specs=pl.BlockSpec(memory_space=pltpu.VMEM),
        scratch_shapes=[
            pltpu.VMEM((n_chunks, response.shape[0], PER_CHUNK * LANES), jnp.bfloat16),
            pltpu.VMEM((factors, species), f32),
            pltpu.VMEM((1, species), jnp.int32),
            pltpu.VMEM((2, nb), f32),
            pltpu.VMEM((nb, LANES, LANES), f32),
            pltpu.VMEM((nb, LANES, LANES), f32),
            pltpu.VMEM((nb, LANES), f32),
            pltpu.VMEM((nb, LANES), f32),
            pltpu.SMEM((2,), jnp.int32),
            pltpu.SMEM((2, 2), jnp.int32),
            pltpu.VMEM((nb, LANES), f32),
            pltpu.VMEM((nb, LANES), f32),
            pltpu.VMEM((nb, LANES), f32),
            pltpu.VMEM((nb, LANES), f32),
            pltpu.VMEM((nb, LANES), f32),
            pltpu.VMEM((n_chunks, factors * PER_CHUNK, LANES), f32),
            pltpu.VMEM((n_chunks, 3, 2 * PER_CHUNK, LANES), f32),
            pltpu.VMEM((n_chunks, PER_CHUNK, LANES), f32),
            pltpu.VMEM((n_chunks, PER_CHUNK, LANES), f32),
            pltpu.VMEM((n_chunks, PER_CHUNK, LANES), f32),
            pltpu.VMEM((region_n, 8, LANES), f32),
            pltpu.VMEM((region_n, 4, LANES), f32),
            dma((7,)),
            dma((n_chunks, runs)),
            dma((n_chunks, runs)),
            dma((n_chunks, runs)),
            dma((n_chunks, 3)),
            dma((n_chunks, 3)),
            dma((n_chunks,)),
            dma((n_chunks,)),
            dma,
            dma,
            dma,
            dma,
        ],
        compiler_params=pltpu.CompilerParams(
            collective_id=0, has_side_effects=True, vmem_limit_bytes=40 * 2**20
        ),
        cost_estimate=pl.CostEstimate(flops=40_000_000, bytes_accessed=13_000_000, transcendentals=0),
        name="sweep",
    )(
        response,
        loadings.T,
        obs_count.reshape(1, species),
        couplings.reshape(nb, 2).T,
        block_cov.reshape(nb, LANES, LANES),
        noise_factor.reshape(nb, LANES, LANES),
        noise.reshape(nb, LANES),
        latents.reshape(nb, LANES),
        colours,
        partners,
    )
    return out.reshape(1, nb * LANES)


def solution(mesh):
    placed = (
        P("factor", "region"),
        P(),
        P(),
        P("factor", "region", None),
        P("factor", "region", None, None),
        P("factor", "region", None, None),
        P("factor", "region"),
        P("factor", "region"),
        P("region"),
        P("region", None),
    )
    return jax.shard_map(
        on_device, mesh=mesh, in_specs=placed, out_specs=P("factor", "region"), check_vma=False
    )
```

```python
import functools
import math

import jax
import jax.numpy as jnp
from jax import lax
from jax.experimental import pallas as pl
from jax.experimental.pallas import tpu as pltpu
from jax.sharding import PartitionSpec as P

MESH = pl.DeviceIdType.MESH
LANES = 128
CHUNKS = (
    ((0, 4), (28, 8), (60, 4)),
    ((4, 16),),
    ((20, 8), (36, 8)),
    ((44, 16),),
)
PER_CHUNK = 16
ENDS = (0, 7, 8, 15)


def kernel(
    species_total,
    resp_hbm,
    load_hbm,
    obs_hbm,
    coup_hbm,
    cov_hbm,
    nf_hbm,
    noise_hbm,
    lat_hbm,
    col_hbm,
    par_hbm,
    out_ref,
    resp_v,
    load_v,
    obs_v,
    coup_v,
    cov_v,
    nf_v,
    noise_v,
    lat_v,
    col_s,
    par_s,
    draw_v,
    local_v,
    field_v,
    c0_v,
    c1_v,
    part_v,
    x_recv,
    z_send,
    z_recv,
    keep_v,
    old_v,
    new_v,
    small_sem,
    resp_sem,
    nf_sem,
    cov_sem,
    x_ssem,
    x_rsem,
    z_ssem,
    z_rsem,
    old_ssem,
    old_rsem,
    new_ssem,
    new_rsem,
):
    n_chunks = len(CHUNKS)
    factors = load_v.shape[0]
    species_local = resp_v.shape[1]
    region_n = lax.axis_size("region")
    ri = lax.axis_index("region")
    fi = lax.axis_index("factor")
    xi = fi // 2
    zi = fi % 2

    small = [
        pltpu.make_async_copy(src, dst, small_sem.at[i])
        for i, (src, dst) in enumerate(
            (
                (load_hbm, load_v),
                (obs_hbm, obs_v),
                (lat_hbm, lat_v),
                (coup_hbm, coup_v),
                (noise_hbm, noise_v),
                (col_hbm, col_s),
                (par_hbm, par_s),
            )
        )
    ]
    for copy in small:
        copy.start()
    resp_in, nf_in, cov_in = [], [], []
    for c, runs in enumerate(CHUNKS):
        at, rows = 0, []
        for i, (first, count) in enumerate(runs):
            rows.append(
                pltpu.make_async_copy(
                    resp_hbm.at[:, pl.ds(first * LANES, count * LANES)],
                    resp_v.at[c, :, pl.ds(at * LANES, count * LANES)],
                    resp_sem.at[c, i],
                )
            )
            at += count
        resp_in.append(rows)
    for hbm, ref, sem, out in ((nf_hbm, nf_v, nf_sem, nf_in), (cov_hbm, cov_v, cov_sem, cov_in)):
        for c, runs in enumerate(CHUNKS):
            at, rows = c * PER_CHUNK, []
            for i, (first, count) in enumerate(runs):
                rows.append(
                    pltpu.make_async_copy(
                        hbm.at[pl.ds(first, count)], ref.at[pl.ds(at, count)], sem.at[c, i]
                    )
                )
                at += count
            out.append(rows)
    for group in (resp_in, nf_in, cov_in):
        for rows in group:
            for copy in rows:
                copy.start()

    x_peers = [lax.rem(xi + d, 4) * 2 + zi for d in (1, 2, 3)]
    z_peer = xi * 2 + (1 - zi)
    barrier = pltpu.get_barrier_semaphore()
    for peer in x_peers + [z_peer]:
        pl.semaphore_signal(barrier, inc=1, device_id={"factor": peer}, device_id_type=MESH)

    @pl.loop(1, region_n)
    def _(d):
        pl.semaphore_signal(
            barrier, inc=1, device_id={"region": lax.rem(ri + d, region_n)}, device_id_type=MESH
        )

    small[0].wait()
    small[1].wait()
    tau = obs_v[...].astype(jnp.float32) * (0.25 / math.sqrt(species_total))
    weighted = load_v[...] * tau
    own_load = load_v[pl.ds(fi, 1), :]
    gram = jnp.sum(weighted * own_load, axis=1, keepdims=True)
    gram = jnp.where(lax.broadcasted_iota(jnp.int32, gram.shape, 0) == fi, 0.0, gram)
    mine = weighted[:, :species_local]
    for k in range(1, factors):
        mine = jnp.where(fi == k, weighted[:, k * species_local : (k + 1) * species_local], mine)
    mine = mine.astype(jnp.bfloat16)
    gram = jnp.broadcast_to(gram, (factors, LANES))

    small[2].wait()
    small[5].wait()
    nb = lat_v.shape[0]
    half = nb // 2
    old_v[ri, pl.ds(0, 1), :] = lat_v[0:1, :]
    old_v[ri, pl.ds(1, 1), :] = lat_v[half - 1 : half, :]
    old_v[ri, pl.ds(2, 1), :] = lat_v[half : half + 1, :]
    old_v[ri, pl.ds(3, 1), :] = lat_v[nb - 1 : nb, :]
    for q in range(2):
        old_v[ri, pl.ds(4 + q, 1), :] = jnp.full((1, LANES), col_s[q].astype(jnp.float32))

    def partial_term(c):
        for copy in resp_in[c]:
            copy.wait()
        term = jnp.dot(mine, resp_v[c], preferred_element_type=jnp.float32)
        at = 0
        for first, count in CHUNKS[c]:
            for k in range(count):
                row = lat_v[first + k : first + k + 1, :]
                value = term[:, at * LANES : (at + 1) * LANES] - gram * row
                part_v[c, pl.ds(at, factors, stride=PER_CHUNK), :] = value
                at += 1

    def x_copies(c):
        copies = []
        for d in range(3):
            start = pl.multiple_of((x_peers[d] - zi) * PER_CHUNK, 2 * PER_CHUNK)
            copies.append(
                pltpu.make_async_remote_copy(
                    src_ref=part_v.at[c, pl.ds(start, 2 * PER_CHUNK)],
                    dst_ref=x_recv.at[c, d],
                    send_sem=x_ssem.at[c, d],
                    recv_sem=x_rsem.at[c, d],
                    device_id={"factor": x_peers[d]},
                    device_id_type=MESH,
                )
            )
        return copies

    def z_copy(c):
        return pltpu.make_async_remote_copy(
            src_ref=z_send.at[c],
            dst_ref=z_recv.at[c],
            send_sem=z_ssem.at[c],
            recv_sem=z_rsem.at[c],
            device_id={"factor": z_peer},
            device_id_type=MESH,
        )

    def send_all(buf, ssem, rsem):
        @pl.loop(1, region_n)
        def _(d):
            pltpu.make_async_remote_copy(
                src_ref=buf.at[ri],
                dst_ref=buf.at[ri],
                send_sem=ssem,
                recv_sem=rsem,
                device_id={"region": lax.rem(ri + d, region_n)},
                device_id_type=MESH,
            ).start()

    def wait_all(buf, sem):
        others = buf.at[pl.ds(0, region_n - 1)]
        pltpu.make_async_copy(others, others, sem).wait()

    partial_term(0)
    pl.semaphore_wait(barrier, 4 + region_n - 1)
    xs = [x_copies(c) for c in range(n_chunks)]
    zs = [z_copy(c) for c in range(n_chunks)]
    for copy in xs[0]:
        copy.start()
    send_all(old_v, old_ssem, old_rsem)
    for c in range(1, n_chunks):
        partial_term(c)
        for copy in xs[c]:
            copy.start()

    diagonal = lax.broadcasted_iota(jnp.int32, (LANES, LANES), 0) == lax.broadcasted_iota(
        jnp.int32, (LANES, LANES), 1
    )

    def times(matrix, row):
        sums = jnp.sum(matrix * row, axis=1, keepdims=True)
        return jnp.sum(jnp.where(diagonal, sums, 0.0), axis=0, keepdims=True)

    small[3].wait()
    pick = lax.broadcasted_iota(jnp.int32, (nb, nb), 0) == lax.broadcasted_iota(
        jnp.int32, (nb, nb), 1
    )
    for i, ref in ((0, c0_v), (1, c1_v)):
        column = jnp.sum(jnp.where(pick, coup_v[i : i + 1, :], 0.0), axis=1, keepdims=True)
        ref[...] = jnp.broadcast_to(column, (nb, LANES))
    rows_at = lax.broadcasted_iota(jnp.int32, (nb, LANES), 0)
    left = pltpu.roll(lat_v[...], 1, 0)
    left = jnp.where((rows_at == 0) | (rows_at == half), 0.0, left)
    right = pltpu.roll(lat_v[...], nb - 1, 0)
    right = jnp.where((rows_at == half - 1) | (rows_at == nb - 1), 0.0, right)
    local_v[...] = c0_v[...] * left + c1_v[...] * right
    small[4].wait()

    def draw(c):
        for copy in nf_in[c]:
            copy.wait()
        at = c * PER_CHUNK
        for first, count in CHUNKS[c]:

            @pl.loop(0, count // 4)
            def _(g, at=at, first=first):
                for k in range(4):
                    row = noise_v[pl.ds(first + 4 * g + k, 1), :]
                    draw_v[pl.ds(first + 4 * g + k, 1), :] = times(nf_v[at + 4 * g + k], row)

            at += count

    def x_sum(c):
        for copy in xs[c]:
            copy.wait_recv()
        at = pl.multiple_of(fi * PER_CHUNK, PER_CHUNK)
        to = pl.multiple_of(z_peer * PER_CHUNK, PER_CHUNK)
        mine_at = pl.multiple_of(zi * PER_CHUNK, PER_CHUNK)
        other_at = pl.multiple_of((1 - zi) * PER_CHUNK, PER_CHUNK)
        out = part_v[c, pl.ds(to, PER_CHUNK), :]
        for d in range(3):
            out = out + x_recv[c, d, pl.ds(other_at, PER_CHUNK), :]
        z_send[c] = out
        zs[c].start()
        own = part_v[c, pl.ds(at, PER_CHUNK), :]
        for d in range(3):
            own = own + x_recv[c, d, pl.ds(mine_at, PER_CHUNK), :]
        keep_v[c] = own

    def z_sum(c):
        zs[c].wait_recv()
        total = keep_v[c] + z_recv[c]
        at = 0
        for first, count in CHUNKS[c]:
            field_v[first : first + count, :] = (
                total[at : at + count, :] + local_v[first : first + count, :]
            )
            at += count

    def blocks(c):
        for copy in cov_in[c]:
            copy.wait()
        at = c * PER_CHUNK
        for first, count in CHUNKS[c]:

            @pl.loop(0, count // 4)
            def _(g, at=at, first=first):
                for k in range(4):
                    b = first + 4 * g + k
                    row = field_v[pl.ds(b, 1), :]
                    out_ref[pl.ds(b, 1), :] = (
                        times(cov_v[at + 4 * g + k], row) + draw_v[pl.ds(b, 1), :]
                    )

            at += count

    def partner_edge(ref, q, side):
        g = par_s[q, side]
        return ref[g // 2, pl.ds(2 * (g % 2) + (1 - side), 1), :]

    def partner_colour(q, side):
        g = par_s[q, side]
        return old_v[g // 2, pl.ds(4 + g % 2, 1), :]

    ends = [
        (q, side, (q * half, q * half + half - 1)[side], ENDS[2 * q + side])
        for q in range(2)
        for side in range(2)
    ]

    draw(0)
    x_sum(0)
    draw(1)
    x_sum(1)
    draw(2)
    z_sum(0)
    small[6].wait()
    for copy in cov_in[0]:
        copy.wait()
    wait_all(old_v, old_rsem)
    for q, side, b, at in ends:
        weight = (c0_v, c1_v)[side][b : b + 1, :]
        row = field_v[b : b + 1, :] + weight * partner_edge(old_v, q, side)
        new_v[ri, pl.ds(2 * q + side, 1), :] = times(cov_v[at], row) + draw_v[b : b + 1, :]
    send_all(new_v, new_ssem, new_rsem)
    x_sum(2)
    draw(3)
    x_sum(3)
    cov_in[0] = []
    for c in range(n_chunks):
        if c:
            z_sum(c)
        blocks(c)
    wait_all(new_v, new_rsem)
    for q, side, b, at in ends:
        weight = (c0_v, c1_v)[side][b : b + 1, :]
        own = jnp.full((1, LANES), col_s[q].astype(jnp.float32))
        edge = jnp.where(
            partner_colour(q, side) < own,
            partner_edge(new_v, q, side),
            partner_edge(old_v, q, side),
        )
        row = field_v[b : b + 1, :] + weight * edge
        out_ref[b : b + 1, :] = times(cov_v[at], row) + draw_v[b : b + 1, :]

    for c in range(n_chunks):
        for copy in xs[c]:
            copy.wait_send()
        zs[c].wait_send()
    wait_all(old_v, old_ssem)
    wait_all(new_v, new_ssem)


def on_device(
    response,
    loadings,
    obs_count,
    couplings,
    block_cov,
    noise_factor,
    noise,
    latents,
    colours,
    partners,
):
    f32 = jnp.float32
    factors = loadings.shape[1]
    species = loadings.shape[0]
    nb = block_cov.shape[1]
    region_n = lax.axis_size("region")
    n_chunks = len(CHUNKS)
    runs = max(len(c) for c in CHUNKS)
    any_spec = pl.BlockSpec(memory_space=pltpu.HBM)
    dma = pltpu.SemaphoreType.DMA
    out = pl.pallas_call(
        functools.partial(kernel, species),
        out_shape=jax.ShapeDtypeStruct((nb, LANES), f32),
        in_specs=[any_spec] * 10,
        out_specs=pl.BlockSpec(memory_space=pltpu.VMEM),
        scratch_shapes=[
            pltpu.VMEM((n_chunks, response.shape[0], PER_CHUNK * LANES), jnp.bfloat16),
            pltpu.VMEM((factors, species), f32),
            pltpu.VMEM((1, species), jnp.int32),
            pltpu.VMEM((2, nb), f32),
            pltpu.VMEM((nb, LANES, LANES), f32),
            pltpu.VMEM((nb, LANES, LANES), f32),
            pltpu.VMEM((nb, LANES), f32),
            pltpu.VMEM((nb, LANES), f32),
            pltpu.SMEM((2,), jnp.int32),
            pltpu.SMEM((2, 2), jnp.int32),
            pltpu.VMEM((nb, LANES), f32),
            pltpu.VMEM((nb, LANES), f32),
            pltpu.VMEM((nb, LANES), f32),
            pltpu.VMEM((nb, LANES), f32),
            pltpu.VMEM((nb, LANES), f32),
            pltpu.VMEM((n_chunks, factors * PER_CHUNK, LANES), f32),
            pltpu.VMEM((n_chunks, 3, 2 * PER_CHUNK, LANES), f32),
            pltpu.VMEM((n_chunks, PER_CHUNK, LANES), f32),
            pltpu.VMEM((n_chunks, PER_CHUNK, LANES), f32),
            pltpu.VMEM((n_chunks, PER_CHUNK, LANES), f32),
            pltpu.VMEM((region_n, 8, LANES), f32),
            pltpu.VMEM((region_n, 4, LANES), f32),
            dma((7,)),
            dma((n_chunks, runs)),
            dma((n_chunks, runs)),
            dma((n_chunks, runs)),
            dma((n_chunks, 3)),
            dma((n_chunks, 3)),
            dma((n_chunks,)),
            dma((n_chunks,)),
            dma,
            dma,
            dma,
            dma,
        ],
        compiler_params=pltpu.CompilerParams(
            collective_id=0, has_side_effects=True, vmem_limit_bytes=60 * 2**20
        ),
        cost_estimate=pl.CostEstimate(flops=40_000_000, bytes_accessed=13_000_000, transcendentals=0),
        name="sweep",
    )(
        response,
        loadings.T,
        obs_count.reshape(1, species),
        couplings.reshape(nb, 2).T,
        block_cov.reshape(nb, LANES, LANES),
        noise_factor.reshape(nb, LANES, LANES),
        noise.reshape(nb, LANES),
        latents.reshape(nb, LANES),
        colours,
        partners,
    )
    return out.reshape(1, nb * LANES)


def solution(mesh):
    placed = (
        P("factor", "region"),
        P(),
        P(),
        P("factor", "region", None),
        P("factor", "region", None, None),
        P("factor", "region", None, None),
        P("factor", "region"),
        P("factor", "region"),
        P("region"),
        P("region", None),
    )
    return jax.shard_map(
        on_device, mesh=mesh, in_specs=placed, out_specs=P("factor", "region"), check_vma=False
    )
```

```python
import functools
import math

import jax
import jax.numpy as jnp
from jax import lax
from jax.experimental import pallas as pl
from jax.experimental.pallas import tpu as pltpu
from jax.sharding import PartitionSpec as P

MESH = pl.DeviceIdType.MESH
LANES = 128
CHUNKS = 4


def kernel(
    species_total,
    resp_hbm,
    load_hbm,
    obs_hbm,
    coup_hbm,
    cov_hbm,
    nf_hbm,
    noise_hbm,
    lat_hbm,
    col_hbm,
    par_hbm,
    out_ref,
    resp_v,
    rend_v,
    load_v,
    obs_v,
    coup_v,
    cov_v,
    nf_v,
    noise_v,
    lat_v,
    col_s,
    par_s,
    draw_v,
    local_v,
    field_v,
    c0_v,
    c1_v,
    part_v,
    x_recv,
    y_recv,
    z_send,
    z_recv,
    end_v,
    end_recv,
    old_v,
    new_v,
    small_sem,
    rend_sem,
    resp_sem,
    nf_sem,
    cov_sem,
    x_ssem,
    x_rsem,
    y_ssem,
    y_rsem,
    z_ssem,
    z_rsem,
    end_ssem,
    end_rsem,
    old_ssem,
    old_rsem,
    new_ssem,
    new_rsem,
):
    factors = load_v.shape[0]
    species_local = resp_v.shape[1]
    nb = lat_v.shape[0]
    half = nb // 2
    per = nb // CHUNKS
    region_n = lax.axis_size("region")
    ri = lax.axis_index("region")
    fi = lax.axis_index("factor")
    xi = fi // 2
    zi = fi % 2
    end_blocks = (0, half - 1, half, nb - 1)

    small = [
        pltpu.make_async_copy(src, dst, small_sem.at[i])
        for i, (src, dst) in enumerate(
            (
                (load_hbm, load_v),
                (obs_hbm, obs_v),
                (lat_hbm, lat_v),
                (coup_hbm, coup_v),
                (noise_hbm, noise_v),
                (col_hbm, col_s),
                (par_hbm, par_s),
            )
        )
    ]
    rend_in = [
        pltpu.make_async_copy(
            resp_hbm.at[:, pl.ds(b * LANES, LANES)],
            rend_v.at[:, pl.ds(i * LANES, LANES)],
            rend_sem.at[i],
        )
        for i, b in enumerate(end_blocks)
    ]
    resp_in = [
        pltpu.make_async_copy(
            resp_hbm.at[:, pl.ds(c * per * LANES, per * LANES)], resp_v.at[c], resp_sem.at[c]
        )
        for c in range(CHUNKS)
    ]
    nf_in, cov_in = (
        [
            pltpu.make_async_copy(
                hbm.at[pl.ds(c * per, per)], ref.at[pl.ds(c * per, per)], sem.at[c]
            )
            for c in range(CHUNKS)
        ]
        for hbm, ref, sem in ((nf_hbm, nf_v, nf_sem), (cov_hbm, cov_v, cov_sem))
    )
    for copy in small[:3] + small[5:6] + rend_in + resp_in:
        copy.start()

    x_peers = [lax.rem(xi + d, 4) * 2 for d in (1, 2, 3)]
    z_peer = xi * 2 + (1 - zi)
    barrier = pltpu.get_barrier_semaphore()
    for d in range(1, factors):
        pl.semaphore_signal(
            barrier, inc=1, device_id={"factor": lax.rem(fi + d, factors)}, device_id_type=MESH
        )

    @pl.loop(1, region_n)
    def _(d):
        pl.semaphore_signal(
            barrier, inc=1, device_id={"region": lax.rem(ri + d, region_n)}, device_id_type=MESH
        )

    for copy in small[3:5] + small[6:]:
        copy.start()

    small[0].wait()
    small[1].wait()
    tau = obs_v[...].astype(jnp.float32) * (0.25 / math.sqrt(species_total))
    weighted = load_v[...] * tau
    own_load = load_v[pl.ds(fi, 1), :]
    gram = jnp.sum(weighted * own_load, axis=1, keepdims=True)
    gram = jnp.where(lax.broadcasted_iota(jnp.int32, gram.shape, 0) == fi, 0.0, gram)
    mine = weighted[:, :species_local]
    for k in range(1, factors):
        mine = jnp.where(fi == k, weighted[:, k * species_local : (k + 1) * species_local], mine)
    mine = mine.astype(jnp.bfloat16)
    gram = jnp.broadcast_to(gram, (factors, LANES))

    small[2].wait()
    small[5].wait()
    for i, b in enumerate(end_blocks):
        old_v[ri, pl.ds(i, 1), :] = lat_v[b : b + 1, :]
    for q in range(2):
        old_v[ri, pl.ds(4 + q, 1), :] = jnp.full((1, LANES), col_s[q].astype(jnp.float32))

    for copy in rend_in:
        copy.wait()
    term = jnp.dot(mine, rend_v[...], preferred_element_type=jnp.float32)
    for i, b in enumerate(end_blocks):
        value = term[:, i * LANES : (i + 1) * LANES] - gram * lat_v[b : b + 1, :]
        end_v[pl.ds(i, factors, stride=8), :] = value

    def send_all(buf, ssem, rsem):
        @pl.loop(1, region_n)
        def _(d):
            pltpu.make_async_remote_copy(
                src_ref=buf.at[ri],
                dst_ref=buf.at[ri],
                send_sem=ssem,
                recv_sem=rsem,
                device_id={"region": lax.rem(ri + d, region_n)},
                device_id_type=MESH,
            ).start()

    def wait_all(buf, sem):
        others = buf.at[pl.ds(0, region_n - 1)]
        pltpu.make_async_copy(others, others, sem).wait()

    pl.semaphore_wait(barrier, factors - 1 + region_n - 1)
    ends_out = []
    for d in range(1, factors):
        peer = lax.rem(fi + d, factors)
        ends_out.append(
            pltpu.make_async_remote_copy(
                src_ref=end_v.at[pl.ds(pl.multiple_of(peer * 8, 8), 8)],
                dst_ref=end_recv.at[d - 1],
                send_sem=end_ssem.at[d - 1],
                recv_sem=end_rsem.at[d - 1],
                device_id={"factor": peer},
                device_id_type=MESH,
            )
        )
    for copy in ends_out:
        copy.start()
    send_all(old_v, old_ssem, old_rsem)

    def rows_of(factor, c):
        return pl.ds(pl.multiple_of(factor * nb + c * per, per), per)

    def x_copies(c):
        return [
            pltpu.make_async_remote_copy(
                src_ref=part_v.at[rows_of(x_peers[d] + 1 - zi, c)],
                dst_ref=x_recv.at[c, d],
                send_sem=x_ssem.at[c, d],
                recv_sem=x_rsem.at[c, d],
                device_id={"factor": x_peers[d] + zi},
                device_id_type=MESH,
            )
            for d in range(3)
        ]

    xs = [x_copies(c) for c in range(CHUNKS)]
    ys = [
        pltpu.make_async_remote_copy(
            src_ref=part_v.at[pl.ds(pl.multiple_of((x_peers[d] + zi) * nb, nb), nb)],
            dst_ref=y_recv.at[d],
            send_sem=y_ssem.at[d],
            recv_sem=y_rsem.at[d],
            device_id={"factor": x_peers[d] + zi},
            device_id_type=MESH,
        )
        for d in range(3)
    ]
    zs = [
        pltpu.make_async_remote_copy(
            src_ref=z_send.at[c],
            dst_ref=z_recv.at[c],
            send_sem=z_ssem.at[c],
            recv_sem=z_rsem.at[c],
            device_id={"factor": z_peer},
            device_id_type=MESH,
        )
        for c in range(CHUNKS)
    ]
    for c in range(CHUNKS):
        resp_in[c].wait()
        nf_in[c].start()
        term = jnp.dot(mine, resp_v[c], preferred_element_type=jnp.float32)
        for i in range(per):
            b = c * per + i
            value = term[:, i * LANES : (i + 1) * LANES] - gram * lat_v[b : b + 1, :]
            part_v[pl.ds(b, factors, stride=nb), :] = value
        for copy in xs[c]:
            copy.start()
    for copy in ys:
        copy.start()

    diagonal = lax.broadcasted_iota(jnp.int32, (LANES, LANES), 0) == lax.broadcasted_iota(
        jnp.int32, (LANES, LANES), 1
    )

    def times(matrix, row):
        sums = jnp.sum(matrix * row, axis=1, keepdims=True)
        return jnp.sum(jnp.where(diagonal, sums, 0.0), axis=0, keepdims=True)

    small[3].wait()
    pick = lax.broadcasted_iota(jnp.int32, (nb, nb), 0) == lax.broadcasted_iota(
        jnp.int32, (nb, nb), 1
    )
    for i, ref in ((0, c0_v), (1, c1_v)):
        column = jnp.sum(jnp.where(pick, coup_v[i : i + 1, :], 0.0), axis=1, keepdims=True)
        ref[...] = jnp.broadcast_to(column, (nb, LANES))
    rows_at = lax.broadcasted_iota(jnp.int32, (nb, LANES), 0)
    left = pltpu.roll(lat_v[...], 1, 0)
    left = jnp.where((rows_at == 0) | (rows_at == half), 0.0, left)
    right = pltpu.roll(lat_v[...], nb - 1, 0)
    right = jnp.where((rows_at == half - 1) | (rows_at == nb - 1), 0.0, right)
    local_v[...] = c0_v[...] * left + c1_v[...] * right
    small[4].wait()

    UNROLL = 8

    def draw(c):
        nf_in[c].wait()
        cov_in[c].start()

        @pl.loop(0, per // UNROLL)
        def _(g):
            for k in range(UNROLL):
                b = c * per + UNROLL * g + k
                draw_v[pl.ds(b, 1), :] = times(nf_v[b], noise_v[pl.ds(b, 1), :])

    def x_sum(c):
        for copy in xs[c]:
            copy.wait_recv()
        out = part_v[rows_of(z_peer, c), :]
        for d in range(3):
            out = out + x_recv[c, d]
        z_send[c] = out
        zs[c].start()

    def z_sum(c):
        zs[c].wait_recv()
        here = pl.ds(c * per, per)
        total = part_v[rows_of(fi, c), :] + local_v[here, :] + z_recv[c]
        for d in range(3):
            total = total + y_recv[d, here, :]
        field_v[here, :] = total

    def blocks(c):
        @pl.loop(0, per // UNROLL)
        def _(g):
            for k in range(UNROLL):
                b = c * per + UNROLL * g + k
                row = field_v[pl.ds(b, 1), :]
                out_ref[pl.ds(b, 1), :] = times(cov_v[b], row) + draw_v[pl.ds(b, 1), :]

    def partner_edge(ref, q, side):
        g = par_s[q, side]
        return ref[g // 2, pl.ds(2 * (g % 2) + (1 - side), 1), :]

    def partner_colour(q, side):
        g = par_s[q, side]
        return old_v[g // 2, pl.ds(4 + g % 2, 1), :]

    draw(0)
    draw(1)
    draw(2)
    for c in range(CHUNKS):
        x_sum(c)
    draw(3)

    for copy in ends_out:
        copy.wait_recv()
    own_end = end_v[pl.ds(pl.multiple_of(fi * 8, 8), 8), :]
    for d in range(factors - 1):
        own_end = own_end + end_recv[d]
    small[6].wait()
    for c in range(CHUNKS):
        cov_in[c].wait()
    wait_all(old_v, old_rsem)
    bases = []
    for i, b in enumerate(end_blocks):
        q, side = i // 2, i % 2
        bases.append(own_end[i : i + 1, :] + local_v[b : b + 1, :])
        weight = (c0_v, c1_v)[side][b : b + 1, :]
        row = bases[i] + weight * partner_edge(old_v, q, side)
        new_v[ri, pl.ds(i, 1), :] = times(cov_v[b], row) + draw_v[b : b + 1, :]
    send_all(new_v, new_ssem, new_rsem)

    for copy in ys:
        copy.wait_recv()
    for c in range(CHUNKS):
        z_sum(c)
        blocks(c)
    wait_all(new_v, new_rsem)
    for i, b in enumerate(end_blocks):
        q, side = i // 2, i % 2
        weight = (c0_v, c1_v)[side][b : b + 1, :]
        own = jnp.full((1, LANES), col_s[q].astype(jnp.float32))
        edge = jnp.where(
            partner_colour(q, side) < own,
            partner_edge(new_v, q, side),
            partner_edge(old_v, q, side),
        )
        row = bases[i] + weight * edge
        out_ref[b : b + 1, :] = times(cov_v[b], row) + draw_v[b : b + 1, :]

    for copy in ends_out + ys + zs + [copy for c in range(CHUNKS) for copy in xs[c]]:
        copy.wait_send()
    wait_all(old_v, old_ssem)
    wait_all(new_v, new_ssem)


def on_device(
    response,
    loadings,
    obs_count,
    couplings,
    block_cov,
    noise_factor,
    noise,
    latents,
    colours,
    partners,
):
    f32 = jnp.float32
    factors = loadings.shape[1]
    species = loadings.shape[0]
    nb = block_cov.shape[1]
    region_n = lax.axis_size("region")
    per = nb // CHUNKS
    any_spec = pl.BlockSpec(memory_space=pltpu.HBM)
    dma = pltpu.SemaphoreType.DMA
    out = pl.pallas_call(
        functools.partial(kernel, species),
        out_shape=jax.ShapeDtypeStruct((nb, LANES), f32),
        in_specs=[any_spec] * 10,
        out_specs=pl.BlockSpec(memory_space=pltpu.VMEM),
        scratch_shapes=[
            pltpu.VMEM((CHUNKS, response.shape[0], per * LANES), jnp.bfloat16),
            pltpu.VMEM((response.shape[0], 4 * LANES), jnp.bfloat16),
            pltpu.VMEM((factors, species), f32),
            pltpu.VMEM((1, species), jnp.int32),
            pltpu.VMEM((2, nb), f32),
            pltpu.VMEM((nb, LANES, LANES), f32),
            pltpu.VMEM((nb, LANES, LANES), f32),
            pltpu.VMEM((nb, LANES), f32),
            pltpu.VMEM((nb, LANES), f32),
            pltpu.SMEM((2,), jnp.int32),
            pltpu.SMEM((2, 2), jnp.int32),
            pltpu.VMEM((nb, LANES), f32),
            pltpu.VMEM((nb, LANES), f32),
            pltpu.VMEM((nb, LANES), f32),
            pltpu.VMEM((nb, LANES), f32),
            pltpu.VMEM((nb, LANES), f32),
            pltpu.VMEM((factors * nb, LANES), f32),
            pltpu.VMEM((CHUNKS, 3, per, LANES), f32),
            pltpu.VMEM((3, nb, LANES), f32),
            pltpu.VMEM((CHUNKS, per, LANES), f32),
            pltpu.VMEM((CHUNKS, per, LANES), f32),
            pltpu.VMEM((factors * 8, LANES), f32),
            pltpu.VMEM((factors - 1, 8, LANES), f32),
            pltpu.VMEM((region_n, 6, LANES), f32),
            pltpu.VMEM((region_n, 4, LANES), f32),
            dma((7,)),
            dma((4,)),
            dma((CHUNKS,)),
            dma((CHUNKS,)),
            dma((CHUNKS,)),
            dma((CHUNKS, 3)),
            dma((CHUNKS, 3)),
            dma((3,)),
            dma((3,)),
            dma((CHUNKS,)),
            dma((CHUNKS,)),
            dma((factors - 1,)),
            dma((factors - 1,)),
            dma,
            dma,
            dma,
            dma,
        ],
        compiler_params=pltpu.CompilerParams(
            collective_id=0, has_side_effects=True, vmem_limit_bytes=60 * 2**20
        ),
        cost_estimate=pl.CostEstimate(flops=40_000_000, bytes_accessed=13_000_000, transcendentals=0),
        name="sweep",
    )(
        response,
        loadings.T,
        obs_count.reshape(1, species),
        couplings.reshape(nb, 2).T,
        block_cov.reshape(nb, LANES, LANES),
        noise_factor.reshape(nb, LANES, LANES),
        noise.reshape(nb, LANES),
        latents.reshape(nb, LANES),
        colours,
        partners,
    )
    return out.reshape(1, nb * LANES)


def solution(mesh):
    placed = (
        P("factor", "region"),
        P(),
        P(),
        P("factor", "region", None),
        P("factor", "region", None, None),
        P("factor", "region", None, None),
        P("factor", "region"),
        P("factor", "region"),
        P("region"),
        P("region", None),
    )
    return jax.shard_map(
        on_device, mesh=mesh, in_specs=placed, out_specs=P("factor", "region"), check_vma=False
    )
```

```python
import functools
import math

import jax
import jax.numpy as jnp
from jax import lax
from jax.experimental import pallas as pl
from jax.experimental.pallas import tpu as pltpu
from jax.sharding import PartitionSpec as P

MESH = pl.DeviceIdType.MESH
LANES = 128
CHUNKS = 4


def kernel(
    species_total,
    resp_hbm,
    load_hbm,
    obs_hbm,
    coup_hbm,
    cov_hbm,
    nf_hbm,
    noise_hbm,
    lat_hbm,
    col_hbm,
    par_hbm,
    out_ref,
    resp_v,
    rend_v,
    load_v,
    obs_v,
    coup_v,
    cov_v,
    nf_v,
    cend_v,
    nend_v,
    noise_v,
    lat_v,
    col_s,
    par_s,
    draw_v,
    local_v,
    field_v,
    c0_v,
    c1_v,
    part_v,
    x_recv,
    y_recv,
    z_send,
    z_recv,
    end_v,
    end_recv,
    old_v,
    new_v,
    small_sem,
    rend_sem,
    cend_sem,
    nend_sem,
    resp_sem,
    nf_sem,
    cov_sem,
    x_ssem,
    x_rsem,
    y_ssem,
    y_rsem,
    z_ssem,
    z_rsem,
    end_ssem,
    end_rsem,
    old_ssem,
    old_rsem,
    new_ssem,
    new_rsem,
):
    factors = load_v.shape[0]
    species_local = resp_v.shape[1]
    nb = lat_v.shape[0]
    half = nb // 2
    per = nb // CHUNKS
    region_n = lax.axis_size("region")
    ri = lax.axis_index("region")
    fi = lax.axis_index("factor")
    xi = fi // 2
    zi = fi % 2
    end_blocks = (0, half - 1, half, nb - 1)

    x_peers = [lax.rem(xi + d, 4) * 2 for d in (1, 2, 3)]
    z_peer = xi * 2 + (1 - zi)
    barrier = pltpu.get_barrier_semaphore()
    for d in range(1, factors):
        pl.semaphore_signal(
            barrier, inc=1, device_id={"factor": lax.rem(fi + d, factors)}, device_id_type=MESH
        )

    small = [
        pltpu.make_async_copy(src, dst, small_sem.at[i])
        for i, (src, dst) in enumerate(
            (
                (load_hbm, load_v),
                (obs_hbm, obs_v),
                (lat_hbm, lat_v),
                (coup_hbm, coup_v),
                (noise_hbm, noise_v),
                (col_hbm, col_s),
                (par_hbm, par_s),
            )
        )
    ]
    rend_in = [
        pltpu.make_async_copy(
            resp_hbm.at[:, pl.ds(b * LANES, LANES)],
            rend_v.at[:, pl.ds(i * LANES, LANES)],
            rend_sem.at[i],
        )
        for i, b in enumerate(end_blocks)
    ]
    resp_in = [
        pltpu.make_async_copy(
            resp_hbm.at[:, pl.ds(c * per * LANES, per * LANES)], resp_v.at[c], resp_sem.at[c]
        )
        for c in range(CHUNKS)
    ]
    nf_in, cov_in = (
        [
            pltpu.make_async_copy(
                hbm.at[pl.ds(c * per, per)], ref.at[pl.ds(c * per, per)], sem.at[c]
            )
            for c in range(CHUNKS)
        ]
        for hbm, ref, sem in ((nf_hbm, nf_v, nf_sem), (cov_hbm, cov_v, cov_sem))
    )
    cend_in, nend_in = (
        [pltpu.make_async_copy(hbm.at[b], ref.at[i], sem.at[i]) for i, b in enumerate(end_blocks)]
        for hbm, ref, sem in ((cov_hbm, cend_v, cend_sem), (nf_hbm, nend_v, nend_sem))
    )
    for copy in small[:3] + rend_in:
        copy.start()

    @pl.loop(1, region_n)
    def _(d):
        pl.semaphore_signal(
            barrier, inc=1, device_id={"region": lax.rem(ri + d, region_n)}, device_id_type=MESH
        )

    for copy in small[3:] + resp_in[:1] + nend_in + cend_in + resp_in[1:]:
        copy.start()

    small[0].wait()
    small[1].wait()
    tau = obs_v[...].astype(jnp.float32) * (0.25 / math.sqrt(species_total))
    weighted = load_v[...] * tau
    own_load = load_v[pl.ds(fi, 1), :]
    gram = jnp.sum(weighted * own_load, axis=1, keepdims=True)
    gram = jnp.where(lax.broadcasted_iota(jnp.int32, gram.shape, 0) == fi, 0.0, gram)
    mine = weighted[:, :species_local]
    for k in range(1, factors):
        mine = jnp.where(fi == k, weighted[:, k * species_local : (k + 1) * species_local], mine)
    mine = mine.astype(jnp.bfloat16)
    gram = jnp.broadcast_to(gram, (factors, LANES))

    small[2].wait()
    small[5].wait()
    for i, b in enumerate(end_blocks):
        old_v[ri, pl.ds(i, 1), :] = lat_v[b : b + 1, :]
    for q in range(2):
        old_v[ri, pl.ds(4 + q, 1), :] = jnp.full((1, LANES), col_s[q].astype(jnp.float32))

    for copy in rend_in:
        copy.wait()
    term = jnp.dot(mine, rend_v[...], preferred_element_type=jnp.float32)
    for i, b in enumerate(end_blocks):
        value = term[:, i * LANES : (i + 1) * LANES] - gram * lat_v[b : b + 1, :]
        for k in range(factors):
            end_v[k, i : i + 1, :] = value[k : k + 1, :]

    def send_all(buf, ssem, rsem):
        @pl.loop(1, region_n)
        def _(d):
            pltpu.make_async_remote_copy(
                src_ref=buf.at[ri],
                dst_ref=buf.at[ri],
                send_sem=ssem,
                recv_sem=rsem,
                device_id={"region": lax.rem(ri + d, region_n)},
                device_id_type=MESH,
            ).start()

    def wait_all(buf, sem):
        others = buf.at[pl.ds(0, region_n - 1)]
        pltpu.make_async_copy(others, others, sem).wait()

    pl.semaphore_wait(barrier, factors - 1 + region_n - 1)
    ends_out = []
    for d in range(1, factors):
        peer = lax.rem(fi + d, factors)
        ends_out.append(
            pltpu.make_async_remote_copy(
                src_ref=end_v.at[peer],
                dst_ref=end_recv.at[d - 1],
                send_sem=end_ssem.at[d - 1],
                recv_sem=end_rsem.at[d - 1],
                device_id={"factor": peer},
                device_id_type=MESH,
            )
        )
    for copy in ends_out:
        copy.start()
    send_all(old_v, old_ssem, old_rsem)

    def rows_of(factor, c):
        return pl.ds(pl.multiple_of(factor * nb + c * per, per), per)

    def x_copies(c):
        return [
            pltpu.make_async_remote_copy(
                src_ref=part_v.at[rows_of(x_peers[d] + 1 - zi, c)],
                dst_ref=x_recv.at[c, d],
                send_sem=x_ssem.at[c, d],
                recv_sem=x_rsem.at[c, d],
                device_id={"factor": x_peers[d] + zi},
                device_id_type=MESH,
            )
            for d in range(3)
        ]

    xs = [x_copies(c) for c in range(CHUNKS)]
    ys = [
        pltpu.make_async_remote_copy(
            src_ref=part_v.at[pl.ds(pl.multiple_of((x_peers[d] + zi) * nb, nb), nb)],
            dst_ref=y_recv.at[d],
            send_sem=y_ssem.at[d],
            recv_sem=y_rsem.at[d],
            device_id={"factor": x_peers[d] + zi},
            device_id_type=MESH,
        )
        for d in range(3)
    ]
    zs = [
        pltpu.make_async_remote_copy(
            src_ref=z_send.at[c],
            dst_ref=z_recv.at[c],
            send_sem=z_ssem.at[c],
            recv_sem=z_rsem.at[c],
            device_id={"factor": z_peer},
            device_id_type=MESH,
        )
        for c in range(CHUNKS)
    ]
    for c in range(CHUNKS):
        resp_in[c].wait()
        nf_in[c].start()
        term = jnp.dot(mine, resp_v[c], preferred_element_type=jnp.float32)
        for i in range(per):
            b = c * per + i
            value = term[:, i * LANES : (i + 1) * LANES] - gram * lat_v[b : b + 1, :]
            part_v[pl.ds(b, factors, stride=nb), :] = value
        for copy in xs[c]:
            copy.start()
    for copy in ys:
        copy.start()

    diagonal = lax.broadcasted_iota(jnp.int32, (LANES, LANES), 0) == lax.broadcasted_iota(
        jnp.int32, (LANES, LANES), 1
    )

    def times(matrix, row):
        sums = jnp.sum(matrix * row, axis=1, keepdims=True)
        return jnp.sum(jnp.where(diagonal, sums, 0.0), axis=0, keepdims=True)

    small[3].wait()
    pick = lax.broadcasted_iota(jnp.int32, (nb, nb), 0) == lax.broadcasted_iota(
        jnp.int32, (nb, nb), 1
    )
    for i, ref in ((0, c0_v), (1, c1_v)):
        column = jnp.sum(jnp.where(pick, coup_v[i : i + 1, :], 0.0), axis=1, keepdims=True)
        ref[...] = jnp.broadcast_to(column, (nb, LANES))
    rows_at = lax.broadcasted_iota(jnp.int32, (nb, LANES), 0)
    left = pltpu.roll(lat_v[...], 1, 0)
    left = jnp.where((rows_at == 0) | (rows_at == half), 0.0, left)
    right = pltpu.roll(lat_v[...], nb - 1, 0)
    right = jnp.where((rows_at == half - 1) | (rows_at == nb - 1), 0.0, right)
    local_v[...] = c0_v[...] * left + c1_v[...] * right
    small[4].wait()

    UNROLL = 8

    def draw(c):
        nf_in[c].wait()
        cov_in[c].start()

        @pl.loop(0, per // UNROLL)
        def _(g):
            for k in range(UNROLL):
                b = c * per + UNROLL * g + k
                draw_v[pl.ds(b, 1), :] = times(nf_v[b], noise_v[pl.ds(b, 1), :])

    def x_sum(c):
        for copy in xs[c]:
            copy.wait_recv()
        out = part_v[rows_of(z_peer, c), :]
        for d in range(3):
            out = out + x_recv[c, d]
        z_send[c] = out
        zs[c].start()

    def z_sum(c):
        zs[c].wait_recv()
        here = pl.ds(c * per, per)
        total = part_v[rows_of(fi, c), :] + local_v[here, :] + z_recv[c]
        for d in range(3):
            total = total + y_recv[d, here, :]
        field_v[here, :] = total

    def blocks(c):
        cov_in[c].wait()

        @pl.loop(0, per // UNROLL)
        def _(g):
            for k in range(UNROLL):
                b = c * per + UNROLL * g + k
                row = field_v[pl.ds(b, 1), :]
                out_ref[pl.ds(b, 1), :] = times(cov_v[b], row) + draw_v[pl.ds(b, 1), :]

    def partner_edge(ref, q, side):
        g = par_s[q, side]
        return ref[g // 2, pl.ds(2 * (g % 2) + (1 - side), 1), :]

    def partner_colour(q, side):
        g = par_s[q, side]
        return old_v[g // 2, pl.ds(4 + g % 2, 1), :]

    end_draws = []
    for i, b in enumerate(end_blocks):
        nend_in[i].wait()
        end_draws.append(times(nend_v[i], noise_v[b : b + 1, :]))
    draw(0)
    draw(1)

    for copy in ends_out:
        copy.wait_recv()
    own_end = end_v[fi]
    for d in range(factors - 1):
        own_end = own_end + end_recv[d]
    small[6].wait()
    for copy in cend_in:
        copy.wait()
    wait_all(old_v, old_rsem)
    bases = []
    for i, b in enumerate(end_blocks):
        q, side = i // 2, i % 2
        bases.append(own_end[i : i + 1, :] + local_v[b : b + 1, :])
        weight = (c0_v, c1_v)[side][b : b + 1, :]
        row = bases[i] + weight * partner_edge(old_v, q, side)
        new_v[ri, pl.ds(i, 1), :] = times(cend_v[i], row) + end_draws[i]
    send_all(new_v, new_ssem, new_rsem)

    for c in range(CHUNKS):
        x_sum(c)
    draw(2)
    draw(3)
    for copy in ys:
        copy.wait_recv()
    for c in range(CHUNKS):
        z_sum(c)
        blocks(c)
    wait_all(new_v, new_rsem)
    for i, b in enumerate(end_blocks):
        q, side = i // 2, i % 2
        weight = (c0_v, c1_v)[side][b : b + 1, :]
        own = jnp.full((1, LANES), col_s[q].astype(jnp.float32))
        edge = jnp.where(
            partner_colour(q, side) < own,
            partner_edge(new_v, q, side),
            partner_edge(old_v, q, side),
        )
        row = bases[i] + weight * edge
        out_ref[b : b + 1, :] = times(cend_v[i], row) + end_draws[i]

    for copy in ends_out + ys + zs + [copy for c in range(CHUNKS) for copy in xs[c]]:
        copy.wait_send()
    wait_all(old_v, old_ssem)
    wait_all(new_v, new_ssem)


def on_device(
    response,
    loadings,
    obs_count,
    couplings,
    block_cov,
    noise_factor,
    noise,
    latents,
    colours,
    partners,
):
    f32 = jnp.float32
    factors = loadings.shape[1]
    species = loadings.shape[0]
    nb = block_cov.shape[1]
    region_n = lax.axis_size("region")
    per = nb // CHUNKS
    any_spec = pl.BlockSpec(memory_space=pltpu.HBM)
    dma = pltpu.SemaphoreType.DMA
    out = pl.pallas_call(
        functools.partial(kernel, species),
        out_shape=pltpu.VMEM((nb, LANES), f32),
        in_specs=[any_spec] * 10,
        out_specs=pl.BlockSpec(memory_space=pltpu.VMEM),
        scratch_shapes=[
            pltpu.VMEM((CHUNKS, response.shape[0], per * LANES), jnp.bfloat16),
            pltpu.VMEM((response.shape[0], 4 * LANES), jnp.bfloat16),
            pltpu.VMEM((factors, species), f32),
            pltpu.VMEM((1, species), jnp.int32),
            pltpu.VMEM((2, nb), f32),
            pltpu.VMEM((nb, LANES, LANES), f32),
            pltpu.VMEM((nb, LANES, LANES), f32),
            pltpu.VMEM((4, LANES, LANES), f32),
            pltpu.VMEM((4, LANES, LANES), f32),
            pltpu.VMEM((nb, LANES), f32),
            pltpu.VMEM((nb, LANES), f32),
            pltpu.SMEM((2,), jnp.int32),
            pltpu.SMEM((2, 2), jnp.int32),
            pltpu.VMEM((nb, LANES), f32),
            pltpu.VMEM((nb, LANES), f32),
            pltpu.VMEM((nb, LANES), f32),
            pltpu.VMEM((nb, LANES), f32),
            pltpu.VMEM((nb, LANES), f32),
            pltpu.VMEM((factors * nb, LANES), f32),
            pltpu.VMEM((CHUNKS, 3, per, LANES), f32),
            pltpu.VMEM((3, nb, LANES), f32),
            pltpu.VMEM((CHUNKS, per, LANES), f32),
            pltpu.VMEM((CHUNKS, per, LANES), f32),
            pltpu.VMEM((factors, 4, LANES), f32),
            pltpu.VMEM((factors - 1, 4, LANES), f32),
            pltpu.VMEM((region_n, 6, LANES), f32),
            pltpu.VMEM((region_n, 4, LANES), f32),
            dma((7,)),
            dma((4,)),
            dma((4,)),
            dma((4,)),
            dma((CHUNKS,)),
            dma((CHUNKS,)),
            dma((CHUNKS,)),
            dma((CHUNKS, 3)),
            dma((CHUNKS, 3)),
            dma((3,)),
            dma((3,)),
            dma((CHUNKS,)),
            dma((CHUNKS,)),
            dma((factors - 1,)),
            dma((factors - 1,)),
            dma,
            dma,
            dma,
            dma,
        ],
        compiler_params=pltpu.CompilerParams(
            collective_id=0, has_side_effects=True, vmem_limit_bytes=60 * 2**20
        ),
        cost_estimate=pl.CostEstimate(flops=40_000_000, bytes_accessed=13_000_000, transcendentals=0),
        name="sweep",
    )(
        response,
        loadings.T,
        obs_count.reshape(1, species),
        couplings.reshape(nb, 2).T,
        block_cov.reshape(nb, LANES, LANES),
        noise_factor.reshape(nb, LANES, LANES),
        noise.reshape(nb, LANES),
        latents.reshape(nb, LANES),
        colours,
        partners,
    )
    return out.reshape(1, nb * LANES)


def solution(mesh):
    placed = (
        P("factor", "region"),
        P(),
        P(),
        P("factor", "region", None),
        P("factor", "region", None, None),
        P("factor", "region", None, None),
        P("factor", "region"),
        P("factor", "region"),
        P("region"),
        P("region", None),
    )
    return jax.shard_map(
        on_device, mesh=mesh, in_specs=placed, out_specs=P("factor", "region"), check_vma=False
    )
```

```python
import functools
import math

import jax
import jax.numpy as jnp
from jax import lax
from jax.experimental import pallas as pl
from jax.experimental.pallas import tpu as pltpu
from jax.sharding import PartitionSpec as P

MESH = pl.DeviceIdType.MESH
LANES = 128
CHUNKS = 4


def kernel(
    species_total,
    resp_hbm,
    load_hbm,
    obs_hbm,
    coup_hbm,
    cov_hbm,
    nf_hbm,
    noise_hbm,
    lat_hbm,
    col_hbm,
    par_hbm,
    out_ref,
    resp_v,
    rend_v,
    load_v,
    obs_v,
    coup_v,
    cov_v,
    nf_v,
    cend_v,
    nend_v,
    noise_v,
    lat_v,
    col_s,
    par_s,
    draw_v,
    local_v,
    field_v,
    c0_v,
    c1_v,
    part_v,
    x_recv,
    y_recv,
    z_send,
    z_recv,
    end_v,
    end_recv,
    old_v,
    new_v,
    small_sem,
    rend_sem,
    cend_sem,
    nend_sem,
    resp_sem,
    nf_sem,
    cov_sem,
    x_ssem,
    x_rsem,
    y_ssem,
    y_rsem,
    z_ssem,
    z_rsem,
    end_ssem,
    end_rsem,
    old_ssem,
    old_rsem,
    new_ssem,
    new_rsem,
):
    factors = load_v.shape[0]
    species_local = resp_v.shape[1]
    nb = lat_v.shape[0]
    half = nb // 2
    per = nb // CHUNKS
    region_n = lax.axis_size("region")
    ri = lax.axis_index("region")
    fi = lax.axis_index("factor")
    xi = fi // 2
    zi = fi % 2
    end_blocks = (0, half - 1, half, nb - 1)

    x_peers = [lax.rem(xi + d, 4) * 2 for d in (1, 2, 3)]
    z_peer = xi * 2 + (1 - zi)
    barrier = pltpu.get_barrier_semaphore()
    for d in range(1, factors):
        pl.semaphore_signal(
            barrier, inc=1, device_id={"factor": lax.rem(fi + d, factors)}, device_id_type=MESH
        )

    small = [
        pltpu.make_async_copy(src, dst, small_sem.at[i])
        for i, (src, dst) in enumerate(
            (
                (load_hbm, load_v),
                (obs_hbm, obs_v),
                (lat_hbm, lat_v),
                (coup_hbm, coup_v),
                (noise_hbm, noise_v),
                (col_hbm, col_s),
                (par_hbm, par_s),
            )
        )
    ]
    rend_in = [
        pltpu.make_async_copy(
            resp_hbm.at[:, pl.ds(b * LANES, LANES)],
            rend_v.at[:, pl.ds(i * LANES, LANES)],
            rend_sem.at[i],
        )
        for i, b in enumerate(end_blocks)
    ]
    resp_in = [
        pltpu.make_async_copy(
            resp_hbm.at[:, pl.ds(c * per * LANES, per * LANES)], resp_v.at[c], resp_sem.at[c]
        )
        for c in range(CHUNKS)
    ]
    nf_in, cov_in = (
        [
            pltpu.make_async_copy(
                hbm.at[pl.ds(c * per, per)], ref.at[pl.ds(c * per, per)], sem.at[c]
            )
            for c in range(CHUNKS)
        ]
        for hbm, ref, sem in ((nf_hbm, nf_v, nf_sem), (cov_hbm, cov_v, cov_sem))
    )
    cend_in, nend_in = (
        [pltpu.make_async_copy(hbm.at[b], ref.at[i], sem.at[i]) for i, b in enumerate(end_blocks)]
        for hbm, ref, sem in ((cov_hbm, cend_v, cend_sem), (nf_hbm, nend_v, nend_sem))
    )
    for copy in small[:3] + rend_in:
        copy.start()

    @pl.loop(1, region_n)
    def _(d):
        pl.semaphore_signal(
            barrier, inc=1, device_id={"region": lax.rem(ri + d, region_n)}, device_id_type=MESH
        )

    for copy in small[3:] + resp_in[:1] + nend_in + cend_in + resp_in[1:]:
        copy.start()

    small[0].wait()
    small[1].wait()
    tau = obs_v[...].astype(jnp.float32) * (0.25 / math.sqrt(species_total))
    weighted = load_v[...] * tau
    own_load = load_v[pl.ds(fi, 1), :]
    gram = jnp.sum(weighted * own_load, axis=1, keepdims=True)
    gram = jnp.where(lax.broadcasted_iota(jnp.int32, gram.shape, 0) == fi, 0.0, gram)
    mine = weighted[:, :species_local]
    for k in range(1, factors):
        mine = jnp.where(fi == k, weighted[:, k * species_local : (k + 1) * species_local], mine)
    mine = mine.astype(jnp.bfloat16)
    gram = jnp.broadcast_to(gram, (factors, LANES))

    small[2].wait()
    small[5].wait()
    for i, b in enumerate(end_blocks):
        old_v[ri, pl.ds(i, 1), :] = lat_v[b : b + 1, :]
    for q in range(2):
        old_v[ri, pl.ds(4 + q, 1), :] = jnp.full((1, LANES), col_s[q].astype(jnp.float32))

    for copy in rend_in:
        copy.wait()
    term = jnp.dot(mine, rend_v[...], preferred_element_type=jnp.float32)
    for i, b in enumerate(end_blocks):
        value = term[:, i * LANES : (i + 1) * LANES] - gram * lat_v[b : b + 1, :]
        for k in range(factors):
            end_v[k, i : i + 1, :] = value[k : k + 1, :]

    def send_all(buf, ssem, rsem):
        for d in sorted(range(1, region_n), key=lambda d: abs(d - region_n // 2)):
            pltpu.make_async_remote_copy(
                src_ref=buf.at[ri],
                dst_ref=buf.at[ri],
                send_sem=ssem,
                recv_sem=rsem,
                device_id={"region": lax.rem(ri + d, region_n)},
                device_id_type=MESH,
            ).start()

    def wait_all(buf, sem):
        others = buf.at[pl.ds(0, region_n - 1)]
        pltpu.make_async_copy(others, others, sem).wait()

    pl.semaphore_wait(barrier, factors - 1 + region_n - 1)
    ends_out = []
    ends_to = [x_peers[d] + 1 - zi for d in (1, 0, 2)] + [z_peer] + [p + zi for p in x_peers]
    for d, peer in enumerate(ends_to, 1):
        ends_out.append(
            pltpu.make_async_remote_copy(
                src_ref=end_v.at[peer],
                dst_ref=end_recv.at[d - 1],
                send_sem=end_ssem.at[d - 1],
                recv_sem=end_rsem.at[d - 1],
                device_id={"factor": peer},
                device_id_type=MESH,
            )
        )
    for copy in ends_out:
        copy.start()
    send_all(old_v, old_ssem, old_rsem)

    def rows_of(factor, c):
        return pl.ds(pl.multiple_of(factor * nb + c * per, per), per)

    def x_copies(c):
        return [
            pltpu.make_async_remote_copy(
                src_ref=part_v.at[rows_of(x_peers[d] + 1 - zi, c)],
                dst_ref=x_recv.at[c, d],
                send_sem=x_ssem.at[c, d],
                recv_sem=x_rsem.at[c, d],
                device_id={"factor": x_peers[d] + zi},
                device_id_type=MESH,
            )
            for d in range(3)
        ]

    xs = [x_copies(c) for c in range(CHUNKS)]
    ys = [
        pltpu.make_async_remote_copy(
            src_ref=part_v.at[pl.ds(pl.multiple_of((x_peers[d] + zi) * nb, nb), nb)],
            dst_ref=y_recv.at[d],
            send_sem=y_ssem.at[d],
            recv_sem=y_rsem.at[d],
            device_id={"factor": x_peers[d] + zi},
            device_id_type=MESH,
        )
        for d in range(3)
    ]
    zs = [
        pltpu.make_async_remote_copy(
            src_ref=z_send.at[c],
            dst_ref=z_recv.at[c],
            send_sem=z_ssem.at[c],
            recv_sem=z_rsem.at[c],
            device_id={"factor": z_peer},
            device_id_type=MESH,
        )
        for c in range(CHUNKS)
    ]
    for c in range(CHUNKS):
        resp_in[c].wait()
        nf_in[c].start()
        term = jnp.dot(mine, resp_v[c], preferred_element_type=jnp.float32)
        for i in range(per):
            b = c * per + i
            value = term[:, i * LANES : (i + 1) * LANES] - gram * lat_v[b : b + 1, :]
            part_v[pl.ds(b, factors, stride=nb), :] = value
        for copy in xs[c]:
            copy.start()
    for copy in ys:
        copy.start()

    diagonal = lax.broadcasted_iota(jnp.int32, (LANES, LANES), 0) == lax.broadcasted_iota(
        jnp.int32, (LANES, LANES), 1
    )

    def times(matrix, row):
        sums = jnp.sum(matrix * row, axis=1, keepdims=True)
        return jnp.sum(jnp.where(diagonal, sums, 0.0), axis=0, keepdims=True)

    small[3].wait()
    pick = lax.broadcasted_iota(jnp.int32, (nb, nb), 0) == lax.broadcasted_iota(
        jnp.int32, (nb, nb), 1
    )
    for i, ref in ((0, c0_v), (1, c1_v)):
        column = jnp.sum(jnp.where(pick, coup_v[i : i + 1, :], 0.0), axis=1, keepdims=True)
        ref[...] = jnp.broadcast_to(column, (nb, LANES))
    rows_at = lax.broadcasted_iota(jnp.int32, (nb, LANES), 0)
    left = pltpu.roll(lat_v[...], 1, 0)
    left = jnp.where((rows_at == 0) | (rows_at == half), 0.0, left)
    right = pltpu.roll(lat_v[...], nb - 1, 0)
    right = jnp.where((rows_at == half - 1) | (rows_at == nb - 1), 0.0, right)
    local_v[...] = c0_v[...] * left + c1_v[...] * right
    small[4].wait()

    UNROLL = 8

    def draw(c):
        nf_in[c].wait()
        cov_in[c].start()

        @pl.loop(0, per // UNROLL)
        def _(g):
            for k in range(UNROLL):
                b = c * per + UNROLL * g + k
                draw_v[pl.ds(b, 1), :] = times(nf_v[b], noise_v[pl.ds(b, 1), :])

    def x_sum(c):
        for copy in xs[c]:
            copy.wait_recv()
        out = part_v[rows_of(z_peer, c), :]
        for d in range(3):
            out = out + x_recv[c, d]
        z_send[c] = out
        zs[c].start()

    def z_sum(c):
        zs[c].wait_recv()
        here = pl.ds(c * per, per)
        total = part_v[rows_of(fi, c), :] + local_v[here, :] + z_recv[c]
        for d in range(3):
            total = total + y_recv[d, here, :]
        field_v[here, :] = total

    def blocks(c):
        cov_in[c].wait()

        @pl.loop(0, per // UNROLL)
        def _(g):
            for k in range(UNROLL):
                b = c * per + UNROLL * g + k
                row = field_v[pl.ds(b, 1), :]
                out_ref[pl.ds(b, 1), :] = times(cov_v[b], row) + draw_v[pl.ds(b, 1), :]

    def partner_edge(ref, q, side):
        g = par_s[q, side]
        return ref[g // 2, pl.ds(2 * (g % 2) + (1 - side), 1), :]

    def partner_colour(q, side):
        g = par_s[q, side]
        return old_v[g // 2, pl.ds(4 + g % 2, 1), :]

    end_draws = []
    for i, b in enumerate(end_blocks):
        nend_in[i].wait()
        end_draws.append(times(nend_v[i], noise_v[b : b + 1, :]))
    draw(0)
    draw(1)
    for c in range(CHUNKS):
        x_sum(c)

    for copy in ends_out:
        copy.wait_recv()
    own_end = end_v[fi]
    for d in range(factors - 1):
        own_end = own_end + end_recv[d]
    small[6].wait()
    for copy in cend_in:
        copy.wait()
    wait_all(old_v, old_rsem)
    bases = []
    for i, b in enumerate(end_blocks):
        q, side = i // 2, i % 2
        bases.append(own_end[i : i + 1, :] + local_v[b : b + 1, :])
        weight = (c0_v, c1_v)[side][b : b + 1, :]
        row = bases[i] + weight * partner_edge(old_v, q, side)
        new_v[ri, pl.ds(i, 1), :] = times(cend_v[i], row) + end_draws[i]
    send_all(new_v, new_ssem, new_rsem)

    draw(2)
    draw(3)
    for copy in ys:
        copy.wait_recv()
    for c in range(CHUNKS):
        z_sum(c)
        blocks(c)
    wait_all(new_v, new_rsem)
    for i, b in enumerate(end_blocks):
        q, side = i // 2, i % 2
        weight = (c0_v, c1_v)[side][b : b + 1, :]
        own = jnp.full((1, LANES), col_s[q].astype(jnp.float32))
        edge = jnp.where(
            partner_colour(q, side) < own,
            partner_edge(new_v, q, side),
            partner_edge(old_v, q, side),
        )
        row = bases[i] + weight * edge
        out_ref[b : b + 1, :] = times(cend_v[i], row) + end_draws[i]

    for copy in ends_out + ys + zs + [copy for c in range(CHUNKS) for copy in xs[c]]:
        copy.wait_send()
    wait_all(old_v, old_ssem)
    wait_all(new_v, new_ssem)


def on_device(
    response,
    loadings,
    obs_count,
    couplings,
    block_cov,
    noise_factor,
    noise,
    latents,
    colours,
    partners,
):
    f32 = jnp.float32
    factors = loadings.shape[1]
    species = loadings.shape[0]
    nb = block_cov.shape[1]
    region_n = lax.axis_size("region")
    per = nb // CHUNKS
    any_spec = pl.BlockSpec(memory_space=pltpu.HBM)
    dma = pltpu.SemaphoreType.DMA
    out = pl.pallas_call(
        functools.partial(kernel, species),
        out_shape=pltpu.VMEM((nb, LANES), f32),
        in_specs=[any_spec] * 10,
        out_specs=pl.BlockSpec(memory_space=pltpu.VMEM),
        scratch_shapes=[
            pltpu.VMEM((CHUNKS, response.shape[0], per * LANES), jnp.bfloat16),
            pltpu.VMEM((response.shape[0], 4 * LANES), jnp.bfloat16),
            pltpu.VMEM((factors, species), f32),
            pltpu.VMEM((1, species), jnp.int32),
            pltpu.VMEM((2, nb), f32),
            pltpu.VMEM((nb, LANES, LANES), f32),
            pltpu.VMEM((nb, LANES, LANES), f32),
            pltpu.VMEM((4, LANES, LANES), f32),
            pltpu.VMEM((4, LANES, LANES), f32),
            pltpu.VMEM((nb, LANES), f32),
            pltpu.VMEM((nb, LANES), f32),
            pltpu.SMEM((2,), jnp.int32),
            pltpu.SMEM((2, 2), jnp.int32),
            pltpu.VMEM((nb, LANES), f32),
            pltpu.VMEM((nb, LANES), f32),
            pltpu.VMEM((nb, LANES), f32),
            pltpu.VMEM((nb, LANES), f32),
            pltpu.VMEM((nb, LANES), f32),
            pltpu.VMEM((factors * nb, LANES), f32),
            pltpu.VMEM((CHUNKS, 3, per, LANES), f32),
            pltpu.VMEM((3, nb, LANES), f32),
            pltpu.VMEM((CHUNKS, per, LANES), f32),
            pltpu.VMEM((CHUNKS, per, LANES), f32),
            pltpu.VMEM((factors, 4, LANES), f32),
            pltpu.VMEM((factors - 1, 4, LANES), f32),
            pltpu.VMEM((region_n, 6, LANES), f32),
            pltpu.VMEM((region_n, 4, LANES), f32),
            dma((7,)),
            dma((4,)),
            dma((4,)),
            dma((4,)),
            dma((CHUNKS,)),
            dma((CHUNKS,)),
            dma((CHUNKS,)),
            dma((CHUNKS, 3)),
            dma((CHUNKS, 3)),
            dma((3,)),
            dma((3,)),
            dma((CHUNKS,)),
            dma((CHUNKS,)),
            dma((factors - 1,)),
            dma((factors - 1,)),
            dma,
            dma,
            dma,
            dma,
        ],
        compiler_params=pltpu.CompilerParams(
            collective_id=0, has_side_effects=True, vmem_limit_bytes=60 * 2**20
        ),
        cost_estimate=pl.CostEstimate(flops=40_000_000, bytes_accessed=13_000_000, transcendentals=0),
        name="sweep",
    )(
        response,
        loadings.T,
        obs_count.reshape(1, species),
        couplings.reshape(nb, 2).T,
        block_cov.reshape(nb, LANES, LANES),
        noise_factor.reshape(nb, LANES, LANES),
        noise.reshape(nb, LANES),
        latents.reshape(nb, LANES),
        colours,
        partners,
    )
    return out.reshape(1, nb * LANES)


def solution(mesh):
    placed = (
        P("factor", "region"),
        P(),
        P(),
        P("factor", "region", None),
        P("factor", "region", None, None),
        P("factor", "region", None, None),
        P("factor", "region"),
        P("factor", "region"),
        P("region"),
        P("region", None),
    )
    return jax.shard_map(
        on_device, mesh=mesh, in_specs=placed, out_specs=P("factor", "region"), check_vma=False
    )
```

```python
import functools
import math

import jax
import jax.numpy as jnp
from jax import lax
from jax.experimental import pallas as pl
from jax.experimental.pallas import tpu as pltpu
from jax.sharding import PartitionSpec as P

MESH = pl.DeviceIdType.MESH
LANES = 128
CHUNKS = 4


def kernel(
    species_total,
    resp_hbm,
    load_hbm,
    obs_hbm,
    coup_hbm,
    cov_hbm,
    nf_hbm,
    noise_hbm,
    lat_hbm,
    col_hbm,
    par_hbm,
    out_ref,
    resp_v,
    rend_v,
    load_v,
    obs_v,
    coup_v,
    cov_v,
    nf_v,
    cend_v,
    nend_v,
    noise_v,
    lat_v,
    col_s,
    par_s,
    draw_v,
    local_v,
    field_v,
    c0_v,
    c1_v,
    part_v,
    x_recv,
    y_recv,
    z_send,
    z_recv,
    end_v,
    end_recv,
    old_v,
    new_v,
    small_sem,
    rend_sem,
    cend_sem,
    nend_sem,
    resp_sem,
    nf_sem,
    cov_sem,
    x_ssem,
    x_rsem,
    y_ssem,
    y_rsem,
    z_ssem,
    z_rsem,
    end_ssem,
    end_rsem,
    old_ssem,
    old_rsem,
    new_ssem,
    new_rsem,
):
    factors = load_v.shape[0]
    species_local = resp_v.shape[1]
    nb = lat_v.shape[0]
    half = nb // 2
    per = nb // CHUNKS
    region_n = lax.axis_size("region")
    ri = lax.axis_index("region")
    fi = lax.axis_index("factor")
    xi = fi // 2
    zi = fi % 2
    end_blocks = (0, half - 1, half, nb - 1)

    x_peers = [lax.rem(xi + d, 4) * 2 for d in (1, 2, 3)]
    z_peer = xi * 2 + (1 - zi)
    barrier = pltpu.get_barrier_semaphore()
    for d in range(1, factors):
        pl.semaphore_signal(
            barrier, inc=1, device_id={"factor": lax.rem(fi + d, factors)}, device_id_type=MESH
        )

    small = [
        pltpu.make_async_copy(src, dst, small_sem.at[i])
        for i, (src, dst) in enumerate(
            (
                (load_hbm, load_v),
                (obs_hbm, obs_v),
                (lat_hbm, lat_v),
                (coup_hbm, coup_v),
                (noise_hbm, noise_v),
                (col_hbm, col_s),
                (par_hbm, par_s),
            )
        )
    ]
    rend_in = [
        pltpu.make_async_copy(
            resp_hbm.at[:, pl.ds(b * LANES, LANES)],
            rend_v.at[:, pl.ds(i * LANES, LANES)],
            rend_sem.at[i],
        )
        for i, b in enumerate(end_blocks)
    ]
    resp_in = [
        pltpu.make_async_copy(
            resp_hbm.at[:, pl.ds(c * per * LANES, per * LANES)], resp_v.at[c], resp_sem.at[c]
        )
        for c in range(CHUNKS)
    ]
    nf_in, cov_in = (
        [
            pltpu.make_async_copy(
                hbm.at[pl.ds(c * per, per)], ref.at[pl.ds(c * per, per)], sem.at[c]
            )
            for c in range(CHUNKS)
        ]
        for hbm, ref, sem in ((nf_hbm, nf_v, nf_sem), (cov_hbm, cov_v, cov_sem))
    )
    cend_in, nend_in = (
        [pltpu.make_async_copy(hbm.at[b], ref.at[i], sem.at[i]) for i, b in enumerate(end_blocks)]
        for hbm, ref, sem in ((cov_hbm, cend_v, cend_sem), (nf_hbm, nend_v, nend_sem))
    )
    for copy in small[:3] + rend_in:
        copy.start()

    @pl.loop(1, region_n)
    def _(d):
        pl.semaphore_signal(
            barrier, inc=1, device_id={"region": lax.rem(ri + d, region_n)}, device_id_type=MESH
        )

    for copy in small[3:] + resp_in[:1] + nend_in + cend_in + resp_in[1:]:
        copy.start()

    small[0].wait()
    small[1].wait()
    tau = obs_v[...].astype(jnp.float32) * (0.25 / math.sqrt(species_total))
    weighted = load_v[...] * tau
    own_load = load_v[pl.ds(fi, 1), :]
    gram = jnp.sum(weighted * own_load, axis=1, keepdims=True)
    gram = jnp.where(lax.broadcasted_iota(jnp.int32, gram.shape, 0) == fi, 0.0, gram)
    mine = weighted[:, :species_local]
    for k in range(1, factors):
        mine = jnp.where(fi == k, weighted[:, k * species_local : (k + 1) * species_local], mine)
    mine = mine.astype(jnp.bfloat16)
    gram = jnp.broadcast_to(gram, (factors, LANES))

    small[2].wait()
    small[5].wait()
    for i, b in enumerate(end_blocks):
        old_v[ri, pl.ds(i, 1), :] = lat_v[b : b + 1, :]
    for q in range(2):
        old_v[ri, pl.ds(4 + q, 1), :] = jnp.full((1, LANES), col_s[q].astype(jnp.float32))

    for copy in rend_in:
        copy.wait()
    term = jnp.dot(mine, rend_v[...], preferred_element_type=jnp.float32)
    for i, b in enumerate(end_blocks):
        value = term[:, i * LANES : (i + 1) * LANES] - gram * lat_v[b : b + 1, :]
        for k in range(factors):
            end_v[k, i : i + 1, :] = value[k : k + 1, :]

    def send_all(buf, ssem, rsem):
        for d in sorted(range(1, region_n), key=lambda d: abs(d - region_n // 2)):
            pltpu.make_async_remote_copy(
                src_ref=buf.at[ri],
                dst_ref=buf.at[ri],
                send_sem=ssem,
                recv_sem=rsem,
                device_id={"region": lax.rem(ri + d, region_n)},
                device_id_type=MESH,
            ).start()

    def wait_all(buf, sem):
        others = buf.at[pl.ds(0, region_n - 1)]
        pltpu.make_async_copy(others, others, sem).wait()

    pl.semaphore_wait(barrier, factors - 1 + region_n - 1)
    ends_out = []
    ends_to = [x_peers[d] + 1 - zi for d in (1, 0, 2)] + [z_peer] + [p + zi for p in x_peers]
    for d, peer in enumerate(ends_to, 1):
        ends_out.append(
            pltpu.make_async_remote_copy(
                src_ref=end_v.at[peer],
                dst_ref=end_recv.at[d - 1],
                send_sem=end_ssem.at[d - 1],
                recv_sem=end_rsem.at[d - 1],
                device_id={"factor": peer},
                device_id_type=MESH,
            )
        )
    for copy in ends_out:
        copy.start()
    send_all(old_v, old_ssem, old_rsem)

    def rows_of(factor, c):
        return pl.ds(pl.multiple_of(factor * nb + c * per, per), per)

    def x_copies(c):
        return [
            pltpu.make_async_remote_copy(
                src_ref=part_v.at[rows_of(x_peers[d] + 1 - zi, c)],
                dst_ref=x_recv.at[c, d],
                send_sem=x_ssem.at[c, d],
                recv_sem=x_rsem.at[c, d],
                device_id={"factor": x_peers[d] + zi},
                device_id_type=MESH,
            )
            for d in range(3)
        ]

    xs = [x_copies(c) for c in range(CHUNKS)]
    ys = [
        pltpu.make_async_remote_copy(
            src_ref=part_v.at[pl.ds(pl.multiple_of((x_peers[d] + zi) * nb, nb), nb)],
            dst_ref=y_recv.at[d],
            send_sem=y_ssem.at[d],
            recv_sem=y_rsem.at[d],
            device_id={"factor": x_peers[d] + zi},
            device_id_type=MESH,
        )
        for d in range(3)
    ]
    zs = [
        pltpu.make_async_remote_copy(
            src_ref=z_send.at[c],
            dst_ref=z_recv.at[c],
            send_sem=z_ssem.at[c],
            recv_sem=z_rsem.at[c],
            device_id={"factor": z_peer},
            device_id_type=MESH,
        )
        for c in range(CHUNKS)
    ]
    for c in range(CHUNKS):
        resp_in[c].wait()
        nf_in[c].start()
        term = jnp.dot(mine, resp_v[c], preferred_element_type=jnp.float32)
        for i in range(per):
            b = c * per + i
            value = term[:, i * LANES : (i + 1) * LANES] - gram * lat_v[b : b + 1, :]
            part_v[pl.ds(b, factors, stride=nb), :] = value
        for copy in xs[c]:
            copy.start()
    for copy in ys:
        copy.start()

    diagonal = lax.broadcasted_iota(jnp.int32, (LANES, LANES), 0) == lax.broadcasted_iota(
        jnp.int32, (LANES, LANES), 1
    )

    def times(matrix, row):
        sums = jnp.sum(matrix * row, axis=1, keepdims=True)
        return jnp.sum(jnp.where(diagonal, sums, 0.0), axis=0, keepdims=True)

    small[3].wait()
    pick = lax.broadcasted_iota(jnp.int32, (nb, nb), 0) == lax.broadcasted_iota(
        jnp.int32, (nb, nb), 1
    )
    for i, ref in ((0, c0_v), (1, c1_v)):
        column = jnp.sum(jnp.where(pick, coup_v[i : i + 1, :], 0.0), axis=1, keepdims=True)
        ref[...] = jnp.broadcast_to(column, (nb, LANES))
    rows_at = lax.broadcasted_iota(jnp.int32, (nb, LANES), 0)
    left = pltpu.roll(lat_v[...], 1, 0)
    left = jnp.where((rows_at == 0) | (rows_at == half), 0.0, left)
    right = pltpu.roll(lat_v[...], nb - 1, 0)
    right = jnp.where((rows_at == half - 1) | (rows_at == nb - 1), 0.0, right)
    local_v[...] = c0_v[...] * left + c1_v[...] * right
    small[4].wait()

    UNROLL = 8

    def draw(c):
        nf_in[c].wait()
        cov_in[c].start()

        @pl.loop(0, per // UNROLL)
        def _(g):
            for k in range(UNROLL):
                b = c * per + UNROLL * g + k
                draw_v[pl.ds(b, 1), :] = times(nf_v[b], noise_v[pl.ds(b, 1), :])

    def x_sum(c):
        for copy in xs[c]:
            copy.wait_recv()
        out = part_v[rows_of(z_peer, c), :]
        for d in range(3):
            out = out + x_recv[c, d]
        z_send[c] = out
        zs[c].start()

    def z_sum(c):
        zs[c].wait_recv()
        here = pl.ds(c * per, per)
        total = part_v[rows_of(fi, c), :] + local_v[here, :] + z_recv[c]
        for d in range(3):
            total = total + y_recv[d, here, :]
        field_v[here, :] = total

    def blocks(c):
        cov_in[c].wait()

        @pl.loop(0, per // UNROLL)
        def _(g):
            for k in range(UNROLL):
                b = c * per + UNROLL * g + k
                row = field_v[pl.ds(b, 1), :]
                out_ref[pl.ds(b, 1), :] = times(cov_v[b], row) + draw_v[pl.ds(b, 1), :]

    def partner_edge(ref, q, side):
        g = par_s[q, side]
        return ref[g // 2, pl.ds(2 * (g % 2) + (1 - side), 1), :]

    def partner_colour(q, side):
        g = par_s[q, side]
        return old_v[g // 2, pl.ds(4 + g % 2, 1), :]

    end_draws = []
    for i, b in enumerate(end_blocks):
        nend_in[i].wait()
        end_draws.append(times(nend_v[i], noise_v[b : b + 1, :]))
    draw(0)
    draw(1)
    for c in range(CHUNKS):
        x_sum(c)

    small[6].wait()
    for copy in cend_in:
        copy.wait()
    wait_all(old_v, old_rsem)
    old_ends, weights = [], []
    for i, b in enumerate(end_blocks):
        q, side = i // 2, i % 2
        old_ends.append(partner_edge(old_v, q, side))
        weights.append((c0_v, c1_v)[side][b : b + 1, :])
    own_end = end_v[fi]
    for copy in ends_out:
        copy.wait_recv()
    for d in range(factors - 1):
        own_end = own_end + end_recv[d]
    bases = []
    for i, b in enumerate(end_blocks):
        bases.append(own_end[i : i + 1, :] + local_v[b : b + 1, :])
        row = bases[i] + weights[i] * old_ends[i]
        new_v[ri, pl.ds(i, 1), :] = times(cend_v[i], row) + end_draws[i]
    send_all(new_v, new_ssem, new_rsem)

    draw(2)
    draw(3)
    for copy in ys:
        copy.wait_recv()
    for c in range(CHUNKS):
        z_sum(c)
        blocks(c)
    for copy in ends_out + ys + zs + [copy for c in range(CHUNKS) for copy in xs[c]]:
        copy.wait_send()
    wait_all(old_v, old_ssem)
    wait_all(new_v, new_ssem)
    later = []
    for i, b in enumerate(end_blocks):
        q, side = i // 2, i % 2
        own = jnp.full((1, LANES), col_s[q].astype(jnp.float32))
        later.append(partner_colour(q, side) < own)
    wait_all(new_v, new_rsem)
    for i, b in enumerate(end_blocks):
        q, side = i // 2, i % 2
        edge = jnp.where(later[i], partner_edge(new_v, q, side), old_ends[i])
        row = bases[i] + weights[i] * edge
        out_ref[b : b + 1, :] = times(cend_v[i], row) + end_draws[i]


def on_device(
    response,
    loadings,
    obs_count,
    couplings,
    block_cov,
    noise_factor,
    noise,
    latents,
    colours,
    partners,
):
    f32 = jnp.float32
    factors = loadings.shape[1]
    species = loadings.shape[0]
    nb = block_cov.shape[1]
    region_n = lax.axis_size("region")
    per = nb // CHUNKS
    any_spec = pl.BlockSpec(memory_space=pltpu.HBM)
    dma = pltpu.SemaphoreType.DMA
    out = pl.pallas_call(
        functools.partial(kernel, species),
        out_shape=pltpu.VMEM((nb, LANES), f32),
        in_specs=[any_spec] * 10,
        out_specs=pl.BlockSpec(memory_space=pltpu.VMEM),
        scratch_shapes=[
            pltpu.VMEM((CHUNKS, response.shape[0], per * LANES), jnp.bfloat16),
            pltpu.VMEM((response.shape[0], 4 * LANES), jnp.bfloat16),
            pltpu.VMEM((factors, species), f32),
            pltpu.VMEM((1, species), jnp.int32),
            pltpu.VMEM((2, nb), f32),
            pltpu.VMEM((nb, LANES, LANES), f32),
            pltpu.VMEM((nb, LANES, LANES), f32),
            pltpu.VMEM((4, LANES, LANES), f32),
            pltpu.VMEM((4, LANES, LANES), f32),
            pltpu.VMEM((nb, LANES), f32),
            pltpu.VMEM((nb, LANES), f32),
            pltpu.SMEM((2,), jnp.int32),
            pltpu.SMEM((2, 2), jnp.int32),
            pltpu.VMEM((nb, LANES), f32),
            pltpu.VMEM((nb, LANES), f32),
            pltpu.VMEM((nb, LANES), f32),
            pltpu.VMEM((nb, LANES), f32),
            pltpu.VMEM((nb, LANES), f32),
            pltpu.VMEM(((factors + 1) * nb, LANES), f32),
            pltpu.VMEM((CHUNKS, 3, per, LANES), f32),
            pltpu.VMEM((3, nb, LANES), f32),
            pltpu.VMEM((CHUNKS, per, LANES), f32),
            pltpu.VMEM((CHUNKS, per, LANES), f32),
            pltpu.VMEM((factors, 4, LANES), f32),
            pltpu.VMEM((factors - 1, 4, LANES), f32),
            pltpu.VMEM((region_n, 6, LANES), f32),
            pltpu.VMEM((region_n, 4, LANES), f32),
            dma((7,)),
            dma((4,)),
            dma((4,)),
            dma((4,)),
            dma((CHUNKS,)),
            dma((CHUNKS,)),
            dma((CHUNKS,)),
            dma((CHUNKS, 3)),
            dma((CHUNKS, 3)),
            dma((3,)),
            dma((3,)),
            dma((CHUNKS,)),
            dma((CHUNKS,)),
            dma((factors - 1,)),
            dma((factors - 1,)),
            dma,
            dma,
            dma,
            dma,
        ],
        compiler_params=pltpu.CompilerParams(
            collective_id=0, has_side_effects=True, vmem_limit_bytes=60 * 2**20
        ),
        cost_estimate=pl.CostEstimate(flops=40_000_000, bytes_accessed=13_000_000, transcendentals=0),
        name="sweep",
    )(
        response,
        loadings.T,
        obs_count.reshape(1, species),
        couplings.reshape(nb, 2).T,
        block_cov.reshape(nb, LANES, LANES),
        noise_factor.reshape(nb, LANES, LANES),
        noise.reshape(nb, LANES),
        latents.reshape(nb, LANES),
        colours,
        partners,
    )
    return out.reshape(1, nb * LANES)


def solution(mesh):
    placed = (
        P("factor", "region"),
        P(),
        P(),
        P("factor", "region", None),
        P("factor", "region", None, None),
        P("factor", "region", None, None),
        P("factor", "region"),
        P("factor", "region"),
        P("region"),
        P("region", None),
    )
    return jax.shard_map(
        on_device, mesh=mesh, in_specs=placed, out_specs=P("factor", "region"), check_vma=False
    )
```

```python
import functools
import math

import jax
import jax.numpy as jnp
from jax import lax
from jax.experimental import pallas as pl
from jax.experimental.pallas import tpu as pltpu
from jax.sharding import PartitionSpec as P

MESH = pl.DeviceIdType.MESH
LANES = 128
CHUNKS = 4


def kernel(
    species_total,
    resp_hbm,
    load_hbm,
    obs_hbm,
    coup_hbm,
    cov_hbm,
    nf_hbm,
    noise_hbm,
    lat_hbm,
    col_hbm,
    par_hbm,
    out_ref,
    resp_v,
    rend_v,
    load_v,
    obs_v,
    coup_v,
    cov_v,
    nf_v,
    cend_v,
    nend_v,
    noise_v,
    lat_v,
    col_s,
    par_s,
    draw_v,
    local_v,
    field_v,
    c0_v,
    c1_v,
    part_v,
    x_recv,
    y_recv,
    z_send,
    z_recv,
    end_v,
    end_recv,
    old_v,
    new_v,
    small_sem,
    rend_sem,
    cend_sem,
    nend_sem,
    resp_sem,
    nf_sem,
    cov_sem,
    x_ssem,
    x_rsem,
    y_ssem,
    y_rsem,
    z_ssem,
    z_rsem,
    end_ssem,
    end_rsem,
    old_ssem,
    old_rsem,
    new_ssem,
    new_rsem,
):
    factors = load_v.shape[0]
    species_local = resp_v.shape[1]
    nb = lat_v.shape[0]
    half = nb // 2
    per = nb // CHUNKS
    region_n = lax.axis_size("region")
    ri = lax.axis_index("region")
    fi = lax.axis_index("factor")
    xi = fi // 2
    zi = fi % 2
    end_blocks = (0, half - 1, half, nb - 1)

    x_peers = [lax.rem(xi + d, 4) * 2 for d in (1, 2, 3)]
    z_peer = xi * 2 + (1 - zi)
    barrier = pltpu.get_barrier_semaphore()
    for d in range(1, factors):
        pl.semaphore_signal(
            barrier, inc=1, device_id={"factor": lax.rem(fi + d, factors)}, device_id_type=MESH
        )

    small = [
        pltpu.make_async_copy(src, dst, small_sem.at[i])
        for i, (src, dst) in enumerate(
            (
                (load_hbm, load_v),
                (obs_hbm, obs_v),
                (lat_hbm, lat_v),
                (coup_hbm, coup_v),
                (noise_hbm, noise_v),
                (col_hbm, col_s),
                (par_hbm, par_s),
            )
        )
    ]
    rend_in = [
        pltpu.make_async_copy(
            resp_hbm.at[:, pl.ds(b * LANES, LANES)],
            rend_v.at[:, pl.ds(i * LANES, LANES)],
            rend_sem.at[i],
        )
        for i, b in enumerate(end_blocks)
    ]
    resp_in = [
        pltpu.make_async_copy(
            resp_hbm.at[:, pl.ds(c * per * LANES, per * LANES)], resp_v.at[c], resp_sem.at[c]
        )
        for c in range(CHUNKS)
    ]
    nf_in, cov_in = (
        [
            pltpu.make_async_copy(
                hbm.at[pl.ds(c * per, per)], ref.at[pl.ds(c * per, per)], sem.at[c]
            )
            for c in range(CHUNKS)
        ]
        for hbm, ref, sem in ((nf_hbm, nf_v, nf_sem), (cov_hbm, cov_v, cov_sem))
    )
    cend_in, nend_in = (
        [pltpu.make_async_copy(hbm.at[b], ref.at[i], sem.at[i]) for i, b in enumerate(end_blocks)]
        for hbm, ref, sem in ((cov_hbm, cend_v, cend_sem), (nf_hbm, nend_v, nend_sem))
    )
    for copy in small[:3] + rend_in:
        copy.start()

    @pl.loop(1, region_n)
    def _(d):
        pl.semaphore_signal(
            barrier, inc=1, device_id={"region": lax.rem(ri + d, region_n)}, device_id_type=MESH
        )

    for copy in small[3:] + resp_in[:1] + nend_in + cend_in + resp_in[1:]:
        copy.start()

    small[0].wait()
    small[1].wait()
    tau = obs_v[...].astype(jnp.float32) * (0.25 / math.sqrt(species_total))
    weighted = load_v[...] * tau
    own_load = load_v[pl.ds(fi, 1), :]
    gram = jnp.sum(weighted * own_load, axis=1, keepdims=True)
    gram = jnp.where(lax.broadcasted_iota(jnp.int32, gram.shape, 0) == fi, 0.0, gram)
    mine = weighted[:, :species_local]
    for k in range(1, factors):
        mine = jnp.where(fi == k, weighted[:, k * species_local : (k + 1) * species_local], mine)
    mine = mine.astype(jnp.bfloat16)
    gram = jnp.broadcast_to(gram, (factors, LANES))

    small[2].wait()
    small[5].wait()
    for i, b in enumerate(end_blocks):
        old_v[ri, pl.ds(i, 1), :] = lat_v[b : b + 1, :]
    for q in range(2):
        old_v[ri, pl.ds(4 + q, 1), :] = jnp.full((1, LANES), col_s[q].astype(jnp.float32))

    for copy in rend_in:
        copy.wait()
    term = jnp.dot(mine, rend_v[...], preferred_element_type=jnp.float32)
    for i, b in enumerate(end_blocks):
        value = term[:, i * LANES : (i + 1) * LANES] - gram * lat_v[b : b + 1, :]
        for k in range(factors):
            end_v[k, i : i + 1, :] = value[k : k + 1, :]

    def send_all(buf, ssem, rsem):
        for d in sorted(range(1, region_n), key=lambda d: abs(d - region_n // 2)):
            pltpu.make_async_remote_copy(
                src_ref=buf.at[ri],
                dst_ref=buf.at[ri],
                send_sem=ssem,
                recv_sem=rsem,
                device_id={"region": lax.rem(ri + d, region_n)},
                device_id_type=MESH,
            ).start()

    def wait_all(buf, sem):
        others = buf.at[pl.ds(0, region_n - 1)]
        pltpu.make_async_copy(others, others, sem).wait()

    pl.semaphore_wait(barrier, factors - 1 + region_n - 1)
    ends_out = []
    ends_to = [x_peers[d] + 1 - zi for d in (1, 0, 2)] + [z_peer] + [p + zi for p in x_peers]
    for d, peer in enumerate(ends_to, 1):
        ends_out.append(
            pltpu.make_async_remote_copy(
                src_ref=end_v.at[peer],
                dst_ref=end_recv.at[d - 1],
                send_sem=end_ssem.at[d - 1],
                recv_sem=end_rsem.at[d - 1],
                device_id={"factor": peer},
                device_id_type=MESH,
            )
        )
    for copy in ends_out:
        copy.start()
    send_all(old_v, old_ssem, old_rsem)

    def rows_of(factor, c):
        return pl.ds(pl.multiple_of(factor * nb + c * per, per), per)

    def x_copies(c):
        return [
            pltpu.make_async_remote_copy(
                src_ref=part_v.at[rows_of(x_peers[d] + 1 - zi, c)],
                dst_ref=x_recv.at[c, d],
                send_sem=x_ssem.at[c, d],
                recv_sem=x_rsem.at[c, d],
                device_id={"factor": x_peers[d] + zi},
                device_id_type=MESH,
            )
            for d in range(3)
        ]

    xs = [x_copies(c) for c in range(CHUNKS)]
    ys = [
        pltpu.make_async_remote_copy(
            src_ref=part_v.at[pl.ds(pl.multiple_of((x_peers[d] + zi) * nb, nb), nb)],
            dst_ref=y_recv.at[d],
            send_sem=y_ssem.at[d],
            recv_sem=y_rsem.at[d],
            device_id={"factor": x_peers[d] + zi},
            device_id_type=MESH,
        )
        for d in range(3)
    ]
    zs = [
        pltpu.make_async_remote_copy(
            src_ref=z_send.at[c],
            dst_ref=z_recv.at[c],
            send_sem=z_ssem.at[c],
            recv_sem=z_rsem.at[c],
            device_id={"factor": z_peer},
            device_id_type=MESH,
        )
        for c in range(CHUNKS)
    ]
    for c in range(CHUNKS):
        resp_in[c].wait()
        nf_in[c].start()
        term = jnp.dot(mine, resp_v[c], preferred_element_type=jnp.float32)
        for i in range(per):
            b = c * per + i
            value = term[:, i * LANES : (i + 1) * LANES] - gram * lat_v[b : b + 1, :]
            part_v[pl.ds(b, factors, stride=nb), :] = value
        for copy in xs[c]:
            copy.start()

    diagonal = lax.broadcasted_iota(jnp.int32, (LANES, LANES), 0) == lax.broadcasted_iota(
        jnp.int32, (LANES, LANES), 1
    )

    def times(matrix, row):
        sums = jnp.sum(matrix * row, axis=1, keepdims=True)
        return jnp.sum(jnp.where(diagonal, sums, 0.0), axis=0, keepdims=True)

    small[3].wait()
    pick = lax.broadcasted_iota(jnp.int32, (nb, nb), 0) == lax.broadcasted_iota(
        jnp.int32, (nb, nb), 1
    )
    for i, ref in ((0, c0_v), (1, c1_v)):
        column = jnp.sum(jnp.where(pick, coup_v[i : i + 1, :], 0.0), axis=1, keepdims=True)
        ref[...] = jnp.broadcast_to(column, (nb, LANES))
    rows_at = lax.broadcasted_iota(jnp.int32, (nb, LANES), 0)
    left = pltpu.roll(lat_v[...], 1, 0)
    left = jnp.where((rows_at == 0) | (rows_at == half), 0.0, left)
    right = pltpu.roll(lat_v[...], nb - 1, 0)
    right = jnp.where((rows_at == half - 1) | (rows_at == nb - 1), 0.0, right)
    local_v[...] = c0_v[...] * left + c1_v[...] * right
    small[4].wait()

    UNROLL = 8

    def draw(c):
        nf_in[c].wait()
        cov_in[c].start()

        @pl.loop(0, per // UNROLL)
        def _(g):
            for k in range(UNROLL):
                b = c * per + UNROLL * g + k
                draw_v[pl.ds(b, 1), :] = times(nf_v[b], noise_v[pl.ds(b, 1), :])

    def x_sum(c):
        for copy in xs[c]:
            copy.wait_recv()
        out = part_v[rows_of(z_peer, c), :]
        for d in range(3):
            out = out + x_recv[c, d]
        z_send[c] = out
        zs[c].start()

    def z_sum(c):
        zs[c].wait_recv()
        here = pl.ds(c * per, per)
        total = part_v[rows_of(fi, c), :] + local_v[here, :] + z_recv[c]
        for d in range(3):
            total = total + y_recv[d, here, :]
        field_v[here, :] = total

    def blocks(c):
        cov_in[c].wait()

        @pl.loop(0, per // UNROLL)
        def _(g):
            for k in range(UNROLL):
                b = c * per + UNROLL * g + k
                row = field_v[pl.ds(b, 1), :]
                out_ref[pl.ds(b, 1), :] = times(cov_v[b], row) + draw_v[pl.ds(b, 1), :]

    def partner_edge(ref, q, side):
        g = par_s[q, side]
        return ref[g // 2, pl.ds(2 * (g % 2) + (1 - side), 1), :]

    def partner_colour(q, side):
        g = par_s[q, side]
        return old_v[g // 2, pl.ds(4 + g % 2, 1), :]

    end_draws = []
    for i, b in enumerate(end_blocks):
        nend_in[i].wait()
        end_draws.append(times(nend_v[i], noise_v[b : b + 1, :]))
    draw(0)
    draw(1)
    for copy in ys:
        copy.start()
    for c in range(CHUNKS):
        x_sum(c)

    small[6].wait()
    for copy in cend_in:
        copy.wait()
    wait_all(old_v, old_rsem)
    old_ends, weights = [], []
    for i, b in enumerate(end_blocks):
        q, side = i // 2, i % 2
        old_ends.append(partner_edge(old_v, q, side))
        weights.append((c0_v, c1_v)[side][b : b + 1, :])
    own_end = end_v[fi]
    for copy in ends_out:
        copy.wait_recv()
    for d in range(factors - 1):
        own_end = own_end + end_recv[d]
    bases = []
    for i, b in enumerate(end_blocks):
        bases.append(own_end[i : i + 1, :] + local_v[b : b + 1, :])
        row = bases[i] + weights[i] * old_ends[i]
        new_v[ri, pl.ds(i, 1), :] = times(cend_v[i], row) + end_draws[i]
    send_all(new_v, new_ssem, new_rsem)

    draw(2)
    draw(3)
    for copy in ys:
        copy.wait_recv()
    for c in range(CHUNKS):
        z_sum(c)
        blocks(c)
    for copy in ends_out + ys + zs + [copy for c in range(CHUNKS) for copy in xs[c]]:
        copy.wait_send()
    wait_all(old_v, old_ssem)
    wait_all(new_v, new_ssem)
    later = []
    for i, b in enumerate(end_blocks):
        q, side = i // 2, i % 2
        own = jnp.full((1, LANES), col_s[q].astype(jnp.float32))
        later.append(partner_colour(q, side) < own)
    wait_all(new_v, new_rsem)
    for i, b in enumerate(end_blocks):
        q, side = i // 2, i % 2
        edge = jnp.where(later[i], partner_edge(new_v, q, side), old_ends[i])
        row = bases[i] + weights[i] * edge
        out_ref[b : b + 1, :] = times(cend_v[i], row) + end_draws[i]


def on_device(
    response,
    loadings,
    obs_count,
    couplings,
    block_cov,
    noise_factor,
    noise,
    latents,
    colours,
    partners,
):
    f32 = jnp.float32
    factors = loadings.shape[1]
    species = loadings.shape[0]
    nb = block_cov.shape[1]
    region_n = lax.axis_size("region")
    per = nb // CHUNKS
    any_spec = pl.BlockSpec(memory_space=pltpu.HBM)
    dma = pltpu.SemaphoreType.DMA
    out = pl.pallas_call(
        functools.partial(kernel, species),
        out_shape=pltpu.VMEM((nb, LANES), f32),
        in_specs=[any_spec] * 10,
        out_specs=pl.BlockSpec(memory_space=pltpu.VMEM),
        scratch_shapes=[
            pltpu.VMEM((CHUNKS, response.shape[0], per * LANES), jnp.bfloat16),
            pltpu.VMEM((response.shape[0], 4 * LANES), jnp.bfloat16),
            pltpu.VMEM((factors, species), f32),
            pltpu.VMEM((1, species), jnp.int32),
            pltpu.VMEM((2, nb), f32),
            pltpu.VMEM((nb, LANES, LANES), f32),
            pltpu.VMEM((nb, LANES, LANES), f32),
            pltpu.VMEM((4, LANES, LANES), f32),
            pltpu.VMEM((4, LANES, LANES), f32),
            pltpu.VMEM((nb, LANES), f32),
            pltpu.VMEM((nb, LANES), f32),
            pltpu.SMEM((2,), jnp.int32),
            pltpu.SMEM((2, 2), jnp.int32),
            pltpu.VMEM((nb, LANES), f32),
            pltpu.VMEM((nb, LANES), f32),
            pltpu.VMEM((nb, LANES), f32),
            pltpu.VMEM((nb, LANES), f32),
            pltpu.VMEM((nb, LANES), f32),
            pltpu.VMEM(((factors + 1) * nb, LANES), f32),
            pltpu.VMEM((CHUNKS, 3, per, LANES), f32),
            pltpu.VMEM((3, nb, LANES), f32),
            pltpu.VMEM((CHUNKS, per, LANES), f32),
            pltpu.VMEM((CHUNKS, per, LANES), f32),
            pltpu.VMEM((factors, 4, LANES), f32),
            pltpu.VMEM((factors - 1, 4, LANES), f32),
            pltpu.VMEM((region_n, 6, LANES), f32),
            pltpu.VMEM((region_n, 4, LANES), f32),
            dma((7,)),
            dma((4,)),
            dma((4,)),
            dma((4,)),
            dma((CHUNKS,)),
            dma((CHUNKS,)),
            dma((CHUNKS,)),
            dma((CHUNKS, 3)),
            dma((CHUNKS, 3)),
            dma((3,)),
            dma((3,)),
            dma((CHUNKS,)),
            dma((CHUNKS,)),
            dma((factors - 1,)),
            dma((factors - 1,)),
            dma,
            dma,
            dma,
            dma,
        ],
        compiler_params=pltpu.CompilerParams(
            collective_id=0, has_side_effects=True, vmem_limit_bytes=60 * 2**20
        ),
        cost_estimate=pl.CostEstimate(flops=40_000_000, bytes_accessed=13_000_000, transcendentals=0),
        name="sweep",
    )(
        response,
        loadings.T,
        obs_count.reshape(1, species),
        couplings.reshape(nb, 2).T,
        block_cov.reshape(nb, LANES, LANES),
        noise_factor.reshape(nb, LANES, LANES),
        noise.reshape(nb, LANES),
        latents.reshape(nb, LANES),
        colours,
        partners,
    )
    return out.reshape(1, nb * LANES)


def solution(mesh):
    placed = (
        P("factor", "region"),
        P(),
        P(),
        P("factor", "region", None),
        P("factor", "region", None, None),
        P("factor", "region", None, None),
        P("factor", "region"),
        P("factor", "region"),
        P("region"),
        P("region", None),
    )
    return jax.shard_map(
        on_device, mesh=mesh, in_specs=placed, out_specs=P("factor", "region"), check_vma=False
    )
```

```python
import functools
import math

import jax
import jax.numpy as jnp
from jax import lax
from jax.experimental import pallas as pl
from jax.experimental.pallas import tpu as pltpu
from jax.sharding import PartitionSpec as P

MESH = pl.DeviceIdType.MESH
LANES = 128
CHUNKS = 4


def kernel(
    species_total,
    resp_hbm,
    load_hbm,
    obs_hbm,
    coup_hbm,
    cov_hbm,
    nf_hbm,
    noise_hbm,
    lat_hbm,
    col_hbm,
    par_hbm,
    out_ref,
    resp_v,
    rend_v,
    load_v,
    obs_v,
    coup_v,
    cov_v,
    nf_v,
    cend_v,
    nend_v,
    noise_v,
    lat_v,
    col_s,
    par_s,
    draw_v,
    local_v,
    field_v,
    c0_v,
    c1_v,
    part_v,
    x_recv,
    y_recv,
    z_send,
    z_recv,
    end_v,
    end_recv,
    old_v,
    new_v,
    small_sem,
    rend_sem,
    cend_sem,
    nend_sem,
    resp_sem,
    nf_sem,
    cov_sem,
    x_ssem,
    x_rsem,
    y_ssem,
    y_rsem,
    z_ssem,
    z_rsem,
    end_ssem,
    end_rsem,
    old_ssem,
    old_rsem,
    new_ssem,
    new_rsem,
):
    factors = load_v.shape[0]
    species_local = resp_v.shape[1]
    nb = lat_v.shape[0]
    half = nb // 2
    per = nb // CHUNKS
    region_n = lax.axis_size("region")
    ri = lax.axis_index("region")
    fi = lax.axis_index("factor")
    xi = fi // 2
    zi = fi % 2
    end_blocks = (0, half - 1, half, nb - 1)

    x_peers = [lax.rem(xi + d, 4) * 2 for d in (1, 2, 3)]
    z_peer = xi * 2 + (1 - zi)
    barrier = pltpu.get_barrier_semaphore()
    for d in range(1, factors):
        pl.semaphore_signal(
            barrier, inc=1, device_id={"factor": lax.rem(fi + d, factors)}, device_id_type=MESH
        )

    small = [
        pltpu.make_async_copy(src, dst, small_sem.at[i])
        for i, (src, dst) in enumerate(
            (
                (load_hbm, load_v),
                (obs_hbm, obs_v),
                (lat_hbm, lat_v),
                (coup_hbm, coup_v),
                (noise_hbm, noise_v),
                (col_hbm, col_s),
                (par_hbm, par_s),
            )
        )
    ]
    rend_in = [
        pltpu.make_async_copy(
            resp_hbm.at[:, pl.ds(b * LANES, LANES)],
            rend_v.at[:, pl.ds(i * LANES, LANES)],
            rend_sem.at[i],
        )
        for i, b in enumerate(end_blocks)
    ]
    resp_in = [
        pltpu.make_async_copy(
            resp_hbm.at[:, pl.ds(c * per * LANES, per * LANES)], resp_v.at[c], resp_sem.at[c]
        )
        for c in range(CHUNKS)
    ]
    nf_in, cov_in = (
        [
            pltpu.make_async_copy(
                hbm.at[pl.ds(c * per, per)], ref.at[pl.ds(c * per, per)], sem.at[c]
            )
            for c in range(CHUNKS)
        ]
        for hbm, ref, sem in ((nf_hbm, nf_v, nf_sem), (cov_hbm, cov_v, cov_sem))
    )
    cend_in, nend_in = (
        [pltpu.make_async_copy(hbm.at[b], ref.at[i], sem.at[i]) for i, b in enumerate(end_blocks)]
        for hbm, ref, sem in ((cov_hbm, cend_v, cend_sem), (nf_hbm, nend_v, nend_sem))
    )
    for copy in small[:3] + rend_in:
        copy.start()

    @pl.loop(1, region_n)
    def _(d):
        pl.semaphore_signal(
            barrier, inc=1, device_id={"region": lax.rem(ri + d, region_n)}, device_id_type=MESH
        )

    for copy in small[3:] + resp_in[:1] + nend_in + cend_in + resp_in[1:]:
        copy.start()

    small[0].wait()
    small[1].wait()
    tau = obs_v[...].astype(jnp.float32) * (0.25 / math.sqrt(species_total))
    weighted = load_v[...] * tau
    own_load = load_v[pl.ds(fi, 1), :]
    gram = jnp.sum(weighted * own_load, axis=1, keepdims=True)
    gram = jnp.where(lax.broadcasted_iota(jnp.int32, gram.shape, 0) == fi, 0.0, gram)
    mine = weighted[:, :species_local]
    for k in range(1, factors):
        mine = jnp.where(fi == k, weighted[:, k * species_local : (k + 1) * species_local], mine)
    mine = mine.astype(jnp.bfloat16)
    gram = jnp.broadcast_to(gram, (factors, LANES))

    small[2].wait()
    small[5].wait()
    for i, b in enumerate(end_blocks):
        old_v[ri, pl.ds(i, 1), :] = lat_v[b : b + 1, :]
    for q in range(2):
        old_v[ri, pl.ds(4 + q, 1), :] = jnp.full((1, LANES), col_s[q].astype(jnp.float32))

    for copy in rend_in:
        copy.wait()
    term = jnp.dot(mine, rend_v[...], preferred_element_type=jnp.float32)
    for i, b in enumerate(end_blocks):
        value = term[:, i * LANES : (i + 1) * LANES] - gram * lat_v[b : b + 1, :]
        for k in range(factors):
            end_v[k, i : i + 1, :] = value[k : k + 1, :]

    def send_all(buf, ssem, rsem):
        for d in sorted(range(1, region_n), key=lambda d: abs(d - region_n // 2)):
            pltpu.make_async_remote_copy(
                src_ref=buf.at[ri],
                dst_ref=buf.at[ri],
                send_sem=ssem,
                recv_sem=rsem,
                device_id={"region": lax.rem(ri + d, region_n)},
                device_id_type=MESH,
            ).start()

    def wait_all(buf, sem):
        others = buf.at[pl.ds(0, region_n - 1)]
        pltpu.make_async_copy(others, others, sem).wait()

    small[3].wait()
    pick = lax.broadcasted_iota(jnp.int32, (nb, nb), 0) == lax.broadcasted_iota(
        jnp.int32, (nb, nb), 1
    )
    for i, ref in ((0, c0_v), (1, c1_v)):
        column = jnp.sum(jnp.where(pick, coup_v[i : i + 1, :], 0.0), axis=1, keepdims=True)
        ref[...] = jnp.broadcast_to(column, (nb, LANES))
    rows_at = lax.broadcasted_iota(jnp.int32, (nb, LANES), 0)
    left = pltpu.roll(lat_v[...], 1, 0)
    left = jnp.where((rows_at == 0) | (rows_at == half), 0.0, left)
    right = pltpu.roll(lat_v[...], nb - 1, 0)
    right = jnp.where((rows_at == half - 1) | (rows_at == nb - 1), 0.0, right)
    local_v[...] = c0_v[...] * left + c1_v[...] * right
    small[4].wait()

    pl.semaphore_wait(barrier, factors - 1 + region_n - 1)
    ends_out = []
    ends_to = [x_peers[d] + 1 - zi for d in (1, 0, 2)] + [z_peer] + [p + zi for p in x_peers]
    for d, peer in enumerate(ends_to, 1):
        ends_out.append(
            pltpu.make_async_remote_copy(
                src_ref=end_v.at[peer],
                dst_ref=end_recv.at[d - 1],
                send_sem=end_ssem.at[d - 1],
                recv_sem=end_rsem.at[d - 1],
                device_id={"factor": peer},
                device_id_type=MESH,
            )
        )
    for copy in ends_out:
        copy.start()
    send_all(old_v, old_ssem, old_rsem)

    def rows_of(factor, c):
        return pl.ds(pl.multiple_of(factor * nb + c * per, per), per)

    def x_copies(c):
        return [
            pltpu.make_async_remote_copy(
                src_ref=part_v.at[rows_of(x_peers[d] + 1 - zi, c)],
                dst_ref=x_recv.at[c, d],
                send_sem=x_ssem.at[c, d],
                recv_sem=x_rsem.at[c, d],
                device_id={"factor": x_peers[d] + zi},
                device_id_type=MESH,
            )
            for d in range(3)
        ]

    xs = [x_copies(c) for c in range(CHUNKS)]
    ys = [
        pltpu.make_async_remote_copy(
            src_ref=part_v.at[pl.ds(pl.multiple_of((x_peers[d] + zi) * nb, nb), nb)],
            dst_ref=y_recv.at[d],
            send_sem=y_ssem.at[d],
            recv_sem=y_rsem.at[d],
            device_id={"factor": x_peers[d] + zi},
            device_id_type=MESH,
        )
        for d in range(3)
    ]
    zs = [
        pltpu.make_async_remote_copy(
            src_ref=z_send.at[c],
            dst_ref=z_recv.at[c],
            send_sem=z_ssem.at[c],
            recv_sem=z_rsem.at[c],
            device_id={"factor": z_peer},
            device_id_type=MESH,
        )
        for c in range(CHUNKS)
    ]
    for c in range(CHUNKS):
        resp_in[c].wait()
        nf_in[c].start()
        term = jnp.dot(mine, resp_v[c], preferred_element_type=jnp.float32)
        for i in range(per):
            b = c * per + i
            value = term[:, i * LANES : (i + 1) * LANES] - gram * lat_v[b : b + 1, :]
            part_v[pl.ds(b, factors, stride=nb), :] = value
        for copy in xs[c]:
            copy.start()
    for copy in ys:
        copy.start()

    diagonal = lax.broadcasted_iota(jnp.int32, (LANES, LANES), 0) == lax.broadcasted_iota(
        jnp.int32, (LANES, LANES), 1
    )

    def times(matrix, row):
        sums = jnp.sum(matrix * row, axis=1, keepdims=True)
        return jnp.sum(jnp.where(diagonal, sums, 0.0), axis=0, keepdims=True)

    UNROLL = 8

    def draw(c):
        nf_in[c].wait()
        cov_in[c].start()

        @pl.loop(0, per // UNROLL)
        def _(g):
            for k in range(UNROLL):
                b = c * per + UNROLL * g + k
                draw_v[pl.ds(b, 1), :] = times(nf_v[b], noise_v[pl.ds(b, 1), :])

    def x_sum(c):
        for copy in xs[c]:
            copy.wait_recv()
        out = part_v[rows_of(z_peer, c), :]
        for d in range(3):
            out = out + x_recv[c, d]
        z_send[c] = out
        zs[c].start()

    def z_sum(c):
        zs[c].wait_recv()
        here = pl.ds(c * per, per)
        total = part_v[rows_of(fi, c), :] + local_v[here, :] + z_recv[c]
        for d in range(3):
            total = total + y_recv[d, here, :]
        field_v[here, :] = total

    def blocks(c):
        cov_in[c].wait()

        @pl.loop(0, per // UNROLL)
        def _(g):
            for k in range(UNROLL):
                b = c * per + UNROLL * g + k
                row = field_v[pl.ds(b, 1), :]
                out_ref[pl.ds(b, 1), :] = times(cov_v[b], row) + draw_v[pl.ds(b, 1), :]

    def partner_edge(ref, q, side):
        g = par_s[q, side]
        return ref[g // 2, pl.ds(2 * (g % 2) + (1 - side), 1), :]

    def partner_colour(q, side):
        g = par_s[q, side]
        return old_v[g // 2, pl.ds(4 + g % 2, 1), :]

    end_draws = []
    for i, b in enumerate(end_blocks):
        nend_in[i].wait()
        end_draws.append(times(nend_v[i], noise_v[b : b + 1, :]))
    draw(0)
    draw(1)
    for c in range(CHUNKS):
        x_sum(c)

    small[6].wait()
    for copy in cend_in:
        copy.wait()
    wait_all(old_v, old_rsem)
    old_ends, weights = [], []
    for i, b in enumerate(end_blocks):
        q, side = i // 2, i % 2
        old_ends.append(partner_edge(old_v, q, side))
        weights.append((c0_v, c1_v)[side][b : b + 1, :])
    own_end = end_v[fi]
    for copy in ends_out:
        copy.wait_recv()
    for d in range(factors - 1):
        own_end = own_end + end_recv[d]
    bases = []
    for i, b in enumerate(end_blocks):
        bases.append(own_end[i : i + 1, :] + local_v[b : b + 1, :])
        row = bases[i] + weights[i] * old_ends[i]
        new_v[ri, pl.ds(i, 1), :] = times(cend_v[i], row) + end_draws[i]
    send_all(new_v, new_ssem, new_rsem)

    draw(2)
    draw(3)
    for copy in ys:
        copy.wait_recv()
    for c in range(CHUNKS):
        z_sum(c)
        blocks(c)
    for copy in ends_out + ys + zs + [copy for c in range(CHUNKS) for copy in xs[c]]:
        copy.wait_send()
    wait_all(old_v, old_ssem)
    wait_all(new_v, new_ssem)
    later = []
    for i, b in enumerate(end_blocks):
        q, side = i // 2, i % 2
        own = jnp.full((1, LANES), col_s[q].astype(jnp.float32))
        later.append(partner_colour(q, side) < own)
    wait_all(new_v, new_rsem)
    for i, b in enumerate(end_blocks):
        q, side = i // 2, i % 2
        edge = jnp.where(later[i], partner_edge(new_v, q, side), old_ends[i])
        row = bases[i] + weights[i] * edge
        out_ref[b : b + 1, :] = times(cend_v[i], row) + end_draws[i]


def on_device(
    response,
    loadings,
    obs_count,
    couplings,
    block_cov,
    noise_factor,
    noise,
    latents,
    colours,
    partners,
):
    f32 = jnp.float32
    factors = loadings.shape[1]
    species = loadings.shape[0]
    nb = block_cov.shape[1]
    region_n = lax.axis_size("region")
    per = nb // CHUNKS
    any_spec = pl.BlockSpec(memory_space=pltpu.HBM)
    dma = pltpu.SemaphoreType.DMA
    out = pl.pallas_call(
        functools.partial(kernel, species),
        out_shape=pltpu.VMEM((nb, LANES), f32),
        in_specs=[any_spec] * 10,
        out_specs=pl.BlockSpec(memory_space=pltpu.VMEM),
        scratch_shapes=[
            pltpu.VMEM((CHUNKS, response.shape[0], per * LANES), jnp.bfloat16),
            pltpu.VMEM((response.shape[0], 4 * LANES), jnp.bfloat16),
            pltpu.VMEM((factors, species), f32),
            pltpu.VMEM((1, species), jnp.int32),
            pltpu.VMEM((2, nb), f32),
            pltpu.VMEM((nb, LANES, LANES), f32),
            pltpu.VMEM((nb, LANES, LANES), f32),
            pltpu.VMEM((4, LANES, LANES), f32),
            pltpu.VMEM((4, LANES, LANES), f32),
            pltpu.VMEM((nb, LANES), f32),
            pltpu.VMEM((nb, LANES), f32),
            pltpu.SMEM((2,), jnp.int32),
            pltpu.SMEM((2, 2), jnp.int32),
            pltpu.VMEM((nb, LANES), f32),
            pltpu.VMEM((nb, LANES), f32),
            pltpu.VMEM((nb, LANES), f32),
            pltpu.VMEM((nb, LANES), f32),
            pltpu.VMEM((nb, LANES), f32),
            pltpu.VMEM(((factors + 1) * nb, LANES), f32),
            pltpu.VMEM((CHUNKS, 3, per, LANES), f32),
            pltpu.VMEM((3, nb, LANES), f32),
            pltpu.VMEM((CHUNKS, per, LANES), f32),
            pltpu.VMEM((CHUNKS, per, LANES), f32),
            pltpu.VMEM((factors, 4, LANES), f32),
            pltpu.VMEM((factors - 1, 4, LANES), f32),
            pltpu.VMEM((region_n, 6, LANES), f32),
            pltpu.VMEM((region_n, 4, LANES), f32),
            dma((7,)),
            dma((4,)),
            dma((4,)),
            dma((4,)),
            dma((CHUNKS,)),
            dma((CHUNKS,)),
            dma((CHUNKS,)),
            dma((CHUNKS, 3)),
            dma((CHUNKS, 3)),
            dma((3,)),
            dma((3,)),
            dma((CHUNKS,)),
            dma((CHUNKS,)),
            dma((factors - 1,)),
            dma((factors - 1,)),
            dma,
            dma,
            dma,
            dma,
        ],
        compiler_params=pltpu.CompilerParams(
            collective_id=0, has_side_effects=True, vmem_limit_bytes=60 * 2**20
        ),
        cost_estimate=pl.CostEstimate(flops=40_000_000, bytes_accessed=13_000_000, transcendentals=0),
        name="sweep",
    )(
        response,
        loadings.T,
        obs_count.reshape(1, species),
        couplings.reshape(nb, 2).T,
        block_cov.reshape(nb, LANES, LANES),
        noise_factor.reshape(nb, LANES, LANES),
        noise.reshape(nb, LANES),
        latents.reshape(nb, LANES),
        colours,
        partners,
    )
    return out.reshape(1, nb * LANES)


def solution(mesh):
    placed = (
        P("factor", "region"),
        P(),
        P(),
        P("factor", "region", None),
        P("factor", "region", None, None),
        P("factor", "region", None, None),
        P("factor", "region"),
        P("factor", "region"),
        P("region"),
        P("region", None),
    )
    return jax.shard_map(
        on_device, mesh=mesh, in_specs=placed, out_specs=P("factor", "region"), check_vma=False
    )
```
